32 devices in a mesh: tm: 8 (over z, core), space: 4 (over y, x).
Axes of the slice: x: 2, y: 2, z: 4, core: 2. Of those that a mesh axis runs over, the one named last changes fastest.
Arguments:
- sections: int32 [8], replicated, may hold values from 1 to 4, 20 in all
- right_side: bfloat16 [32, 64, 2048], P('tm'), may hold values from -6 to 6
- tip_side: float32 [64, 8], replicated, may hold values from -48 to 48
- diag_inverse: bfloat16 [32, 2048, 2048], P('tm', 'space'), may hold values from -0.08 to 0.42, as said below
- forward_coupling: bfloat16 [32, 2048, 128], P('tm', 'space'), may hold values from -1 to 1
- backward_coupling: bfloat16 [32, 2048, 128], P('tm', 'space'), may hold values from -1 to 1
- arrow_rows: bfloat16 [32, 8, 2048], P('tm', None, 'space'), may hold values from -3.3 to 3.3
- tip_inverse: float32 [8, 8], replicated, may hold values from -0.4 to 0.4, as said below
Outputs:
- solution: float32 [32, 64, 2048], P('tm', None, 'space')
- tip_solution: float32 [64, 8], replicated
The draws below stay inside these ranges and needn't reach their ends.
Inputs may be any that keep to these rules, and one draw needn't show every extreme that they name: Section i holds the live slots i * 4 to i * 4 + sections[i] - 1. `diag_inverse`: each block is lower triangular with a positive diagonal. `tip_inverse`: lower triangular with a positive diagonal.
All inputs are finite; a program needn't handle non-finite values.
Results may differ from the reference program's by a relative error of at most 0.0031.
Values sent between devices are 32-bit elements; how exact they have to be, the bound alone decides.
A program may use at most 64 MiB of HBM per device.

```python
import math
import jax
import jax.numpy as jnp
import numpy as np
from jax import lax

S = 2048
SUB = 128
F = 8
RHS = 64
CAP = 4
SLOTS = 32
TBLK = 20
N_TM = 8


def rough_field(key, shape):
    return jax.random.normal(key, shape, jnp.float32)


def draw_diag_inverse(key, part):
    key_rough = jax.random.fold_in(key, 13)
    key_diag = jax.random.fold_in(key, 31)
    indices = jnp.arange(S)
    below_diag = indices[:, None] > indices[None, :]
    on_diagonal = indices[:, None] == indices[None, :]
    diagonal = jax.random.uniform(key_diag, (SLOTS, S), jnp.float32, 0.6, 1.4)
    slot_keys = jax.random.split(key_rough, SLOTS)

    def one_slot(pair):
        slot_key, diag_row = pair
        rough = jnp.clip(rough_field(slot_key, (S, S)), -4.0, 4.0)
        combined = jnp.where(below_diag, 0.5 * rough / jnp.sqrt(S * 1.0), 0.0) + jnp.where(on_diagonal, diag_row[:, None], 0.0)
        return (0.3 * combined).astype(jnp.bfloat16)
    return lax.map(one_slot, (slot_keys, diagonal))


def draw_forward_coupling(key, part):
    rough = jnp.clip(rough_field(jax.random.fold_in(key, 11), (SLOTS, S, SUB)), -2.0, 2.0)
    return (0.96 * rough / jnp.sqrt(SUB * 1.0)).astype(jnp.bfloat16)


def draw_backward_coupling(key, part):
    rough = jnp.clip(rough_field(jax.random.fold_in(key, 12), (SLOTS, S, SUB)), -2.0, 2.0)
    return (0.96 * rough / jnp.sqrt(SUB * 1.0)).astype(jnp.bfloat16)


def draw_arrow_rows(key, part):
    rough = jnp.clip(rough_field(jax.random.fold_in(key, 14), (SLOTS, F, S)), -4.0, 4.0)
    slot_ramp = 0.6 * 3.0 ** (jnp.arange(SLOTS, dtype=jnp.float32) / (SLOTS - 1))
    row_scale = 32.0 / jnp.sqrt(TBLK * S * 1.0)
    scaled = jnp.clip(row_scale * slot_ramp[:, None, None] * rough, -3.25, 3.25)
    return scaled.astype(jnp.bfloat16)


def draw_tip_inverse(key, part):
    key_rough = jax.random.fold_in(key, 15)
    key_diag = jax.random.fold_in(key, 51)
    indices = jnp.arange(F)
    below_diag = indices[:, None] > indices[None, :]
    on_diagonal = indices[:, None] == indices[None, :]
    rough = jnp.clip(rough_field(key_rough, (F, F)), -4.0, 4.0)
    diagonal = jax.random.uniform(key_diag, (F,), jnp.float32, 0.8, 1.2)
    combined = jnp.where(below_diag, 0.3 * rough, 0.0) + jnp.where(on_diagonal, diagonal[:, None], 0.0)
    return 0.17 * combined


def block_scale(own_key, shape, pieces, least, top_value):
    def one(axis_at, parts):
        heights = jax.random.uniform(jax.random.fold_in(jax.random.fold_in(own_key, 6), axis_at), (parts,), jnp.float32, least / len(pieces), top_value / len(pieces))
        return jnp.repeat(jnp.exp(heights), shape[axis_at] // parts).reshape((-1,) + (1,) * (len(shape) - axis_at - 1))

    level = one(*pieces[0])
    for cut in pieces[1:]:
        level = level * one(*cut)
    return level


def profile(count, total, reach, lean):
    portions = [(1 << 20) // math.isqrt(rank ** lean) + 1 for rank in range(2, count + 1)]
    surplus, holding = total - reach - (count - 1), [1] * (count - 1)
    while surplus > 0:
        candidates = [i for i in range(count - 1) if holding[i] < reach]
        pool, left = sum([portions[i] for i in candidates]), surplus
        for i in candidates:
            addition = min(reach - holding[i], max(1, left * portions[i] // pool), surplus)
            holding[i] = holding[i] + addition
            surplus = surplus - addition
    return np.array([reach] + holding)


def uneven(own_key, count, total, limit, skew):
    if count == 2:
        one = jax.random.randint(own_key, (), max(1, total - limit), min(limit, total - 1) + 1)
        return jnp.stack([one, total - one])
    sizes = jnp.asarray(profile(count, total, limit, skew), jnp.int32)
    twos = (count - 1) // 2
    source_of, taker = sizes[1:1 + 2 * twos:2], sizes[2:2 + 2 * twos:2]
    slack = jnp.minimum(source_of - 1, limit - taker)
    shifted = jax.random.randint(jax.random.fold_in(own_key, 1), (twos,), 0, 1 << 20) % (slack + 1)
    sizes = sizes.at[1:1 + 2 * twos:2].set(source_of - shifted).at[2:2 + 2 * twos:2].set(taker + shifted)
    return sizes[jax.random.permutation(jax.random.fold_in(own_key, 2), count)]


def scatter_about(stream_key, shape, spread, reach, cuts=(), held_as=jnp.bfloat16):
    values = spread * jax.random.normal(stream_key, shape, jnp.float32)
    if cuts:
        values = values * block_scale(stream_key, shape, cuts, -0.22, 0.18)
    return jnp.clip(values, -reach, reach).astype(held_as)


def setup_inputs(seed: int = 0) -> dict:
    key_list = jax.random.split(jax.random.key(seed), 9)
    return {
        "sections": uneven(key_list[0], N_TM, N_TM * 5 // 2, CAP, 2).astype(jnp.int32),
        "right_side": scatter_about(key_list[1], (SLOTS, RHS, S), 1.0, 6.0, ((0, 8),)),
        "tip_side": scatter_about(key_list[2], (RHS, F), 8.0, 48.0, (), jnp.float32),
        "diag_inverse": draw_diag_inverse(jax.random.fold_in(key_list[8], 71), 0),
        "forward_coupling": draw_forward_coupling(jax.random.fold_in(key_list[8], 71), 0),
        "backward_coupling": draw_backward_coupling(jax.random.fold_in(key_list[8], 71), 0),
        "arrow_rows": draw_arrow_rows(jax.random.fold_in(key_list[8], 71), 0),
        "tip_inverse": draw_tip_inverse(jax.random.fold_in(key_list[8], 71), 0),
    }


def couple(states, coupling):
    row_count = states.shape[0]
    sub_count = S // SUB
    shaped = states.reshape(row_count, sub_count, SUB)
    blocks = coupling.astype(jnp.float32).reshape(sub_count, SUB, SUB)
    return jnp.einsum("rnk,nik->rni", shaped, blocks, precision=lax.Precision.HIGHEST).reshape(row_count, S)


def reference(sections, right_side, tip_side, diag_inverse, forward_coupling, backward_coupling, arrow_rows, tip_inverse):
    slot_ids = jnp.arange(SLOTS, dtype=jnp.int32)
    live_slot = (slot_ids % CAP) < jnp.repeat(sections, CAP)

    def forward_step(carried, inputs):
        side_block, inverse_block, coupling_block, live_flag = inputs
        driven = jnp.dot(side_block, inverse_block.T, preferred_element_type=jnp.float32)
        update = driven - couple(carried, coupling_block)
        state = jnp.where(live_flag, update, jnp.float32(0.0))
        carried = jnp.where(live_flag, update, carried)
        return carried, state

    start = jnp.zeros((RHS, S), jnp.float32)
    _, forward_state = lax.scan(forward_step, start, (right_side, diag_inverse, forward_coupling, live_slot))
    arrow_wide = arrow_rows.astype(jnp.float32)
    arrow_total = jnp.einsum("trs,tfs->rf", forward_state.astype(jnp.bfloat16).astype(jnp.float32), arrow_wide, precision=lax.Precision.HIGHEST)
    tip_state = jnp.dot(tip_side - arrow_total, tip_inverse.T, precision=lax.Precision.HIGHEST)
    tip_solution = jnp.dot(tip_state, tip_inverse, precision=lax.Precision.HIGHEST)
    backward_source = (forward_state - jnp.einsum("rf,tfs->trs", tip_solution, arrow_wide, precision=lax.Precision.HIGHEST)).astype(jnp.bfloat16)

    def backward_step(following, inputs):
        source_block, inverse_block, coupling_block, live_flag = inputs
        source = jnp.dot(source_block, inverse_block, preferred_element_type=jnp.float32)
        update = source - couple(following, coupling_block)
        state = jnp.where(live_flag, update, jnp.float32(0.0))
        following = jnp.where(live_flag, update, following)
        return following, state

    _, solution = lax.scan(backward_step, start, (backward_source, diag_inverse, backward_coupling, live_slot), reverse=True)
    return solution, tip_solution
```

```python
import functools

import jax
import jax.numpy as jnp
from jax import lax
from jax.experimental import pallas as pl
from jax.experimental.pallas import tpu as pltpu
from jax.sharding import PartitionSpec as P

F32 = jnp.float32
BF16 = jnp.bfloat16
MESH = pl.DeviceIdType.MESH


def dot(a, b, contract):
    return lax.dot_general(a, b, (contract, ((), ())), preferred_element_type=F32)


def stacked(x):
    high = x.astype(BF16).astype(F32)
    return jnp.concatenate([high, x - high], 0).astype(BF16)


def folded(y):
    rows = y.shape[0] // 2
    return y[:rows] + y[rows:]


def couple(x, block):
    return folded(dot(stacked(x), block, ((1,), (1,))))


def apply_map(x, high, low):
    rows = x.shape[0]
    pieces = stacked(x)
    return folded(dot(pieces, high, ((1,), (0,)))) + dot(pieces[:rows], low, ((1,), (0,)))


def kernel(
    n_tm, n_sp, sec, rs, tip_side, diag_hbm, fc, bc, arrow, tip_inv,
    sol, tip_out,
    diag, fmap_h, fmap_l, bmap_h, bmap_l, driven, f_in, f_out, f_split,
    w_send, w_recv, v_send, v_recv, g_loc, b_in, b_out, part, gath_sp, gath_tm, mine_tm,
    diag_sem, fs_sem, fr_sem, bs_sem, br_sem, ws_sem, wr_sem, vs_sem, vr_sem,
    as_sem, ar_sem, ts_sem, tr_sem,
):
    T, rows = rs.shape[0], rs.shape[1]
    width, sub = fc.shape[1], fc.shape[2]
    nsub = width // sub
    F = arrow.shape[1]
    s, p = lax.axis_index("tm"), lax.axis_index("space")
    length = sec[s]

    loads = [
        pltpu.make_async_copy(diag_hbm.at[t], diag.at[t], diag_sem.at[t]) for t in range(T)
    ]
    for load in loads:
        load.start()

    barrier = pltpu.get_barrier_semaphore()
    for d in range(1, n_tm):
        pl.semaphore_signal(barrier, inc=1, device_id={"tm": lax.rem(s + d, n_tm)}, device_id_type=MESH)
    for d in range(1, n_sp):
        pl.semaphore_signal(barrier, inc=1, device_id={"space": lax.rem(p + d, n_sp)}, device_id_type=MESH)

    def cols(n):
        return slice(n * sub, (n + 1) * sub)

    def select(t, new, old):
        if t == 0:
            return new
        return jnp.where(jnp.full(new.shape, length, jnp.int32) > t, new, old)

    def remote(src, dst, send, recv, to):
        return pltpu.make_async_remote_copy(
            src_ref=src, dst_ref=dst, send_sem=send, recv_sem=recv, device_id=to, device_id_type=MESH
        )

    def section_maps(coupling, order, high_ref, low_ref):
        row = lax.broadcasted_iota(jnp.int32, (sub, sub), 0)
        col = lax.broadcasted_iota(jnp.int32, (sub, sub), 1)
        eye = jnp.where(row == col, 1.0, 0.0).astype(F32)
        maps = [eye] * nsub
        for t in order:
            for n in range(nsub):
                maps[n] = select(t, -couple(maps[n], coupling[t, cols(n), :]), maps[n])
                high = maps[n].astype(BF16)
                high_ref[n, :, cols(t)] = high
                low_ref[n, :, cols(t)] = (maps[n] - high.astype(F32)).astype(BF16)

    section_maps(fc, range(T), fmap_h, fmap_l)
    carry = [None] * nsub
    for t in range(T):
        loads[t].wait()
        full = dot(rs[t], diag[t], ((1,), (1,)))
        for n in range(nsub):
            new = full[:, cols(n)]
            if t > 0:
                new = select(t, new - couple(carry[n], fc[t, cols(n), :]), carry[n])
            carry[n] = new
            driven[t, n] = new

    pl.semaphore_wait(barrier, n_tm - 1 + n_sp - 1)

    def arrow_products():
        for q in range(n_sp - 1):

            @pl.when(p > q)
            def _():
                for t in range(T):
                    full = dot(arrow[t], diag[t, :, q * width : (q + 1) * width], ((1,), (0,)))
                    for n in range(nsub):
                        v_send[q, t, n] = full[:, cols(n)]
                remote(v_send.at[q], v_recv.at[p - 1], vs_sem.at[q], vr_sem.at[p - 1], {"space": q}).start()

    def early():
        arrow_products()
        section_maps(bc, range(T - 1, -1, -1), bmap_h, bmap_l)

    pl.when(s >= n_tm // 2)(early)

    def chain(first, last, to, arrived, leaving, ssem, rsem, own, high, low, at):
        @pl.when(first)
        def _():
            arrived[...] = jnp.zeros(arrived.shape, F32)

        for n in range(nsub):
            hop = remote(leaving.at[n], arrived.at[n], ssem.at[n], rsem.at[n], {"tm": to})
            pl.when(jnp.logical_not(first))(hop.wait_recv)

            @pl.when(jnp.logical_not(last))
            def _():
                leaving[n] = own[at, n] + apply_map(
                    arrived[n], high[n, :, cols(at)], low[n, :, cols(at)]
                )
                hop.start()

    def chain_end(last, to, arrived, leaving, ssem, rsem):
        @pl.when(jnp.logical_not(last))
        def _():
            for n in range(nsub):
                remote(leaving.at[n], arrived.at[n], ssem.at[n], rsem.at[n], {"tm": to}).wait_send()

    f_first, f_last, f_to = s == 0, s == n_tm - 1, lax.rem(s + 1, n_tm)
    chain(f_first, f_last, f_to, f_in, f_out, fs_sem, fr_sem, driven, fmap_h, fmap_l, T - 1)

    for n in range(nsub):
        states = apply_map(f_in[n], fmap_h[n], fmap_l[n])
        for t in range(T):
            state = driven[t, n] + states[:, cols(t)]
            state = select(t, state, jnp.zeros_like(state))
            f_split[t, :, cols(n)] = stacked(state)

    for q in range(n_sp - 1):

        @pl.when(p > q)
        def _():
            for t in range(T - 1, -1, -1):
                full = folded(dot(f_split[t], diag[t, :, q * width : (q + 1) * width], ((1,), (0,))))
                for n in range(nsub):
                    w_send[q, t, n] = full[:, cols(n)]
                remote(
                    w_send.at[q, t], w_recv.at[p - 1, t], ws_sem.at[q, t], wr_sem.at[p - 1, t], {"space": q}
                ).start()

    total = jnp.zeros((F, 2 * rows), F32)
    for t in range(T):
        total = total + dot(arrow[t], f_split[t], ((1,), (1,)))
    part[...] = total
    gath_sp[p] = total
    for d in range(1, n_sp):
        remote(part, gath_sp.at[p], as_sem.at[d - 1], ar_sem.at[p], {"space": lax.rem(p + d, n_sp)}).start()

    pl.when(s < n_tm // 2)(early)

    for d in range(1, n_sp):
        come = lax.rem(p + d, n_sp)
        remote(part, gath_sp.at[come], as_sem.at[d - 1], ar_sem.at[come], {"space": come}).wait_recv()
    total = gath_sp[0]
    for i in range(1, n_sp):
        total = total + gath_sp[i]
    mine_tm[...] = total
    gath_tm[s] = total
    for d in range(1, n_tm):
        remote(mine_tm, gath_tm.at[s], ts_sem.at[d - 1], tr_sem.at[s], {"tm": lax.rem(s + d, n_tm)}).start()

    own_cols = pl.ds(pl.multiple_of(p * width, width), width)
    for t in range(T):
        block = diag[t, :, own_cols]
        full = folded(dot(f_split[t], block, ((1,), (0,))))
        arrow_full = dot(arrow[t], block, ((1,), (0,)))
        for n in range(nsub):
            g_loc[t, n, :rows] = full[:, cols(n)]
            g_loc[t, n, rows:] = arrow_full[:, cols(n)]
    for q in range(1, n_sp):

        @pl.when(p < q)
        def _():
            remote(v_send.at[0], v_recv.at[q - 1], vs_sem.at[0], vr_sem.at[q - 1], {"space": q}).wait_recv()
            for t in range(T):
                for n in range(nsub):
                    g_loc[t, n, rows:] += v_recv[q - 1, t, n]

    for t in range(T - 1, -1, -1):
        for q in range(1, n_sp):

            @pl.when(p < q)
            def _():
                remote(
                    w_send.at[0, t], w_recv.at[q - 1, t], ws_sem.at[0, t], wr_sem.at[q - 1, t], {"space": q}
                ).wait_recv()
                for n in range(nsub):
                    g_loc[t, n, :rows] += w_recv[q - 1, t, n]

        for n in range(nsub):
            new = g_loc[t, n]
            if t < T - 1:
                old = g_loc[t + 1, n]
                new = select(t, new - couple(old, bc[t, cols(n), :]), old)
            else:
                new = select(t, new, jnp.zeros_like(new))
            g_loc[t, n] = new

    b_first, b_last, b_to = s == n_tm - 1, s == 0, lax.rem(s + n_tm - 1, n_tm)
    chain(b_first, b_last, b_to, b_in, b_out, bs_sem, br_sem, g_loc, bmap_h, bmap_l, 0)

    for d in range(1, n_tm):
        come = lax.rem(s + d, n_tm)
        remote(mine_tm, gath_tm.at[come], ts_sem.at[d - 1], tr_sem.at[come], {"tm": come}).wait_recv()
    total = gath_tm[0]
    for i in range(1, n_tm):
        total = total + gath_tm[i]
    exact = functools.partial(
        lax.dot_general, preferred_element_type=F32, precision=lax.Precision.HIGHEST
    )
    side = tip_side[...] - total.T[:rows, :]
    tip_state = exact(side, tip_inv[...], (((1,), (1,)), ((), ())))
    tip = exact(tip_state, tip_inv[...], (((1,), (0,)), ((), ())))
    tip_out[...] = tip

    for n in range(nsub):
        states = apply_map(b_in[n], bmap_h[n], bmap_l[n])
        for t in range(T):
            state = g_loc[t, n] + states[:, cols(t)]
            value = state[:rows] - exact(tip, state[rows:], (((1,), (0,)), ((), ())))
            sol[t, :, cols(n)] = select(t, value, jnp.zeros_like(value))

    chain_end(f_last, f_to, f_in, f_out, fs_sem, fr_sem)
    chain_end(b_last, b_to, b_in, b_out, bs_sem, br_sem)
    for q in range(n_sp - 1):

        @pl.when(p > q)
        def _():
            remote(v_send.at[q], v_recv.at[p - 1], vs_sem.at[q], vr_sem.at[p - 1], {"space": q}).wait_send()
            for t in range(T):
                remote(
                    w_send.at[q, t], w_recv.at[p - 1, t], ws_sem.at[q, t], wr_sem.at[p - 1, t], {"space": q}
                ).wait_send()

    for d in range(1, n_sp):
        remote(part, gath_sp.at[p], as_sem.at[d - 1], ar_sem.at[p], {"space": lax.rem(p + d, n_sp)}).wait_send()
    for d in range(1, n_tm):
        remote(mine_tm, gath_tm.at[s], ts_sem.at[d - 1], tr_sem.at[s], {"tm": lax.rem(s + d, n_tm)}).wait_send()


def on_device(n_tm, n_sp, sections, right_side, tip_side, diag_inverse, fwd, bwd, arrow_rows, tip_inverse):
    T, rows, total_width = right_side.shape
    width, sub = fwd.shape[1], fwd.shape[2]
    nsub = width // sub
    F = arrow_rows.shape[1]
    both = rows + F
    vmem = pl.BlockSpec(memory_space=pltpu.VMEM)
    maps = pltpu.VMEM((nsub, sub, T * sub), BF16)
    dma = pltpu.SemaphoreType.DMA
    others = n_sp - 1
    return pl.pallas_call(
        functools.partial(kernel, n_tm, n_sp),
        out_shape=(
            jax.ShapeDtypeStruct((T, rows, width), F32),
            jax.ShapeDtypeStruct(tip_side.shape, F32),
        ),
        in_specs=[
            pl.BlockSpec(memory_space=pltpu.SMEM),
            vmem,
            vmem,
            pl.BlockSpec(memory_space=pl.ANY),
            vmem,
            vmem,
            vmem,
            vmem,
        ],
        out_specs=(vmem, vmem),
        scratch_shapes=[
            pltpu.VMEM(diag_inverse.shape, BF16),
            maps,
            maps,
            maps,
            maps,
            pltpu.VMEM((T, nsub, rows, sub), F32),
            pltpu.VMEM((nsub, rows, sub), F32),
            pltpu.VMEM((nsub, rows, sub), F32),
            pltpu.VMEM((T, 2 * rows, width), BF16),
            pltpu.VMEM((others, T, nsub, rows, sub), F32),
            pltpu.VMEM((others, T, nsub, rows, sub), F32),
            pltpu.VMEM((others, T, nsub, F, sub), F32),
            pltpu.VMEM((others, T, nsub, F, sub), F32),
            pltpu.VMEM((T, nsub, both, sub), F32),
            pltpu.VMEM((nsub, both, sub), F32),
            pltpu.VMEM((nsub, both, sub), F32),
            pltpu.VMEM((F, 2 * rows), F32),
            pltpu.VMEM((n_sp, F, 2 * rows), F32),
            pltpu.VMEM((n_tm, F, 2 * rows), F32),
            pltpu.VMEM((F, 2 * rows), F32),
            dma((T,)),
            dma((nsub,)),
            dma((nsub,)),
            dma((nsub,)),
            dma((nsub,)),
            dma((others, T)),
            dma((others, T)),
            dma((others,)),
            dma((others,)),
            dma((others,)),
            dma((n_sp,)),
            dma((n_tm - 1,)),
            dma((n_tm,)),
        ],
        compiler_params=pltpu.CompilerParams(
            collective_id=0, has_side_effects=True, vmem_limit_bytes=56 * 1024 * 1024
        ),
        cost_estimate=pl.CostEstimate(
            flops=8 * T * rows * width * total_width, bytes_accessed=2 * diag_inverse.size, transcendentals=0
        ),
    )(sections, right_side, tip_side, diag_inverse, fwd, bwd, arrow_rows, tip_inverse)


def solution(mesh):
    placed = (
        P(),
        P("tm", None, None),
        P(),
        P("tm", "space", None),
        P("tm", "space", None),
        P("tm", "space", None),
        P("tm", None, "space"),
        P(),
    )
    return jax.shard_map(
        functools.partial(on_device, mesh.shape["tm"], mesh.shape["space"]),
        mesh=mesh,
        in_specs=placed,
        out_specs=(P("tm", None, "space"), P()),
        check_vma=False,
    )
```

```python
import functools

import jax
import jax.numpy as jnp
from jax import lax
from jax.experimental import pallas as pl
from jax.experimental.pallas import tpu as pltpu
from jax.sharding import PartitionSpec as P

F32 = jnp.float32
BF16 = jnp.bfloat16
MESH = pl.DeviceIdType.MESH


def dot(a, b, contract):
    return lax.dot_general(a, b, (contract, ((), ())), preferred_element_type=F32)


def stacked(x):
    high = x.astype(BF16).astype(F32)
    return jnp.concatenate([high, x - high], 0).astype(BF16)


def folded(y):
    rows = y.shape[0] // 2
    return y[:rows] + y[rows:]


def couple(x, block):
    return folded(dot(stacked(x), block, ((1,), (1,))))


def apply_map(x, high, low):
    rows = x.shape[0]
    pieces = stacked(x)
    return folded(dot(pieces, high, ((1,), (0,)))) + dot(pieces[:rows], low, ((1,), (0,)))


def kernel(
    n_tm, n_sp, sec, rs, tip_side, diag_hbm, fc, bc, arrow, tip_inv,
    sol, tip_out,
    diag, fmap_h, fmap_l, bmap_h, bmap_l, driven, f_split, g_loc,
    w_send, w_recv, w_pass, v_send, v_recv, part, gath_sp, gath_tm, mine_tm,
    f_scan, b_scan,
    diag_sem, ws_sem, wr_sem, ps_sem, pr_sem, vs_sem, vr_sem, as_sem, ar_sem, ts_sem, tr_sem,
):
    T, rows = rs.shape[0], rs.shape[1]
    width, sub = fc.shape[1], fc.shape[2]
    nsub = width // sub
    F = arrow.shape[1]
    s, p = lax.axis_index("tm"), lax.axis_index("space")
    core, chip, chips = lax.rem(s, 2), s // 2, n_tm // 2
    length = sec[s]
    half, split = (nsub // 2, True) if nsub % 2 == 0 else (nsub, False)
    base = core * half if split else 0
    other_base = half - core * half if split else 0
    mate = s + 1 - 2 * core

    loads = [
        pltpu.make_async_copy(diag_hbm.at[t], diag.at[t], diag_sem.at[t]) for t in range(T)
    ]
    for load in loads:
        load.start()

    barrier = pltpu.get_barrier_semaphore()
    for d in range(1, n_tm):
        pl.semaphore_signal(barrier, inc=1, device_id={"tm": lax.rem(s + d, n_tm)}, device_id_type=MESH)
    for d in range(1, n_sp):
        pl.semaphore_signal(barrier, inc=1, device_id={"space": lax.rem(p + d, n_sp)}, device_id_type=MESH)

    def cols(n):
        return slice(n * sub, (n + 1) * sub)

    def select(t, new, old):
        if t == 0:
            return new
        return jnp.where(jnp.full(new.shape, length, jnp.int32) > t, new, old)

    def remote(src, dst, send, recv, to):
        return pltpu.make_async_remote_copy(
            src_ref=src, dst_ref=dst, send_sem=send, recv_sem=recv, device_id=to, device_id_type=MESH
        )

    def section_maps(coupling, order, high_ref, low_ref, own_map):
        row = lax.broadcasted_iota(jnp.int32, (sub, sub), 0)
        col = lax.broadcasted_iota(jnp.int32, (sub, sub), 1)
        eye = jnp.where(row == col, 1.0, 0.0).astype(F32)
        maps = [eye] * nsub
        for t in order:
            for n in range(nsub):
                maps[n] = select(t, -couple(maps[n], coupling[t, cols(n), :]), maps[n])
                high = maps[n].astype(BF16)
                high_ref[n, :, cols(t)] = high
                low_ref[n, :, cols(t)] = (maps[n] - high.astype(F32)).astype(BF16)
        for n in range(nsub):
            own_map[n] = maps[n]

    def in_order(mine, theirs, lead):
        ahead = jnp.full(mine.shape, core, jnp.int32) == lead
        return jnp.where(ahead, mine, theirs), jnp.where(ahead, theirs, mine)

    def map_copy(scan):
        return remote(
            scan["map"].at[pl.ds(other_base, half)], scan["mate_map"],
            scan["sem"].at[0, 0], scan["sem"].at[1, 0], {"tm": mate},
        )

    def off_copy(scan, own):
        return remote(
            own.at[pl.ds(other_base, half)], scan["mate_off"],
            scan["sem"].at[0, 1], scan["sem"].at[1, 1], {"tm": mate},
        )

    def join_maps(scan, lead):
        map_copy(scan).wait_recv()
        for j in range(half):
            one, two = in_order(scan["map"][base + j], scan["mate_map"][j], lead)
            high = two.astype(BF16)
            both = apply_map(one, high, (two - high.astype(F32)).astype(BF16))
            for i, value in enumerate((both, one)):
                high = value.astype(BF16)
                scan["join_h"][j, :, cols(i)] = high
                scan["join_l"][j, :, cols(i)] = (value - high.astype(F32)).astype(BF16)
            scan["two"][j] = two

    def join_offsets(scan, own, lead):
        off_copy(scan, own).wait_recv()
        for j in range(half):
            one, two = in_order(own[base + j], scan["mate_off"][j], lead)
            after = scan["two"][j]
            high = after.astype(BF16)
            scan["join_off"][j, :, cols(0)] = two + apply_map(one, high, (after - high.astype(F32)).astype(BF16))
            scan["join_off"][j, :, cols(1)] = one

    def hop_copy(scan, j, to):
        return remote(
            scan["out"].at[j], scan["arrived"].at[j],
            scan["sem"].at[0, 2 + j], scan["sem"].at[1, 2 + j], {"tm": to},
        )

    def hand_copy(scan, j, at):
        return remote(
            scan["hand"].at[j], scan["into"].at[at + j],
            scan["sem"].at[0, 2 + half + j], scan["sem"].at[1, 2 + half + j], {"tm": mate},
        )

    def chain(scan, first, last, to, lead):
        @pl.when(first)
        def _():
            scan["arrived"][...] = jnp.zeros(scan["arrived"].shape, F32)

        for j in range(half):
            pl.when(jnp.logical_not(first))(hop_copy(scan, j, to).wait_recv)
            arrived = scan["arrived"][j]
            after = scan["join_off"][j] + apply_map(arrived, scan["join_h"][j], scan["join_l"][j])
            scan["out"][j] = after[:, :sub]
            pl.when(jnp.logical_not(last))(hop_copy(scan, j, to).start)
            mine, theirs = in_order(arrived, after[:, sub:], lead)
            scan["into"][base + j] = mine
            if split:
                scan["hand"][j] = theirs
                hand_copy(scan, j, base).start()
        if split:
            for j in range(half):
                hand_copy(scan, j, other_base).wait_recv()

    def scan_end(scan, own, last, to):
        map_copy(scan).wait_send()
        off_copy(scan, own).wait_send()
        for j in range(half):
            pl.when(jnp.logical_not(last))(hop_copy(scan, j, to).wait_send)
            if split:
                hand_copy(scan, j, base).wait_send()

    f_first, f_last, f_to = chip == 0, chip == chips - 1, lax.rem(s + 2, n_tm)
    b_first, b_last, b_to = f_last, f_first, lax.rem(s + n_tm - 2, n_tm)

    section_maps(fc, range(T), fmap_h, fmap_l, f_scan["map"])
    pl.semaphore_wait(barrier, n_tm - 1 + n_sp - 1)
    map_copy(f_scan).start()
    carry = [None] * nsub
    for t in range(T):
        loads[t].wait()
        full = dot(rs[t], diag[t], ((1,), (1,)))
        for n in range(nsub):
            new = full[:, cols(n)]
            if t > 0:
                new = select(t, new - couple(carry[n], fc[t, cols(n), :]), carry[n])
            carry[n] = new
            driven[t, n] = new
    off_copy(f_scan, driven.at[T - 1]).start()
    join_maps(f_scan, 0)
    join_offsets(f_scan, driven.at[T - 1], 0)

    def early():
        section_maps(bc, range(T - 1, -1, -1), bmap_h, bmap_l, b_scan["map"])
        map_copy(b_scan).start()
        for q in range(n_sp - 1):

            @pl.when(p > q)
            def _():
                for t in range(T):
                    full = dot(arrow[t], diag[t, :, q * width : (q + 1) * width], ((1,), (0,)))
                    for n in range(nsub):
                        v_send[q, t, n] = full[:, cols(n)]
                remote(v_send.at[q], v_recv.at[p - 1], vs_sem.at[q], vr_sem.at[p - 1], {"space": q}).start()

    pl.when(chip >= chips // 2)(early)

    chain(f_scan, f_first, f_last, f_to, 0)

    for n in range(nsub):
        states = apply_map(f_scan["into"][n], fmap_h[n], fmap_l[n])
        for t in range(T):
            state = driven[t, n] + states[:, cols(t)]
            state = select(t, state, jnp.zeros_like(state))
            f_split[t, :, cols(n)] = stacked(state)

    down = range(T - 1, -1, -1)
    merging = n_sp == 4 and nsub % 2 == 0
    mid = nsub // 2

    def product(q, t):
        full = folded(dot(f_split[t], diag[t, :, q * width : (q + 1) * width], ((1,), (0,))))
        for n in range(nsub):
            w_send[q, t, n] = full[:, cols(n)]

    def piece(h):
        return pl.ds(0, nsub) if h is None else pl.ds(h * mid, mid)

    def final(q, t, slot, h):
        sem = h or 0
        return remote(
            w_send.at[q, t, piece(h)], w_recv.at[slot, t, piece(h)],
            ws_sem.at[q, t, sem], wr_sem.at[slot, t, sem], {"space": q},
        )

    def passing(q, t, to, h):
        return remote(
            w_send.at[q, t, piece(h)], w_pass.at[t, piece(h)],
            ps_sem.at[t, h or 0], pr_sem.at[t], {"space": to},
        )

    def merge(q, t, h):
        passing(q, t, 0, h).wait_recv()
        for n in range(nsub) if h is None else range(h * mid, h * mid + mid):
            w_send[q, t, n] += w_pass[t, n]

    if merging:

        @pl.when(p == 3)
        def _():
            for t in down:
                product(0, t)
                passing(0, t, 2, 0).start()
                passing(0, t, 1, 1).start()
            for t in down:
                product(2, t)
                final(2, t, 0, None).start()
                product(1, t)
                merge(1, t, None)
                final(1, t, 0, None).start()

        @pl.when(p == 2)
        def _():
            for t in down:
                product(1, t)
                passing(1, t, 3, None).start()
                product(0, t)
                final(0, t, 1, 1).start()
            for t in down:
                merge(0, t, 0)
                final(0, t, 1, 0).start()

        @pl.when(p == 1)
        def _():
            for t in down:
                product(0, t)
                final(0, t, 0, 0).start()
            for t in down:
                merge(0, t, 1)
                final(0, t, 0, 1).start()

    else:
        for q in range(n_sp - 1):

            @pl.when(p > q)
            def _():
                for t in down:
                    product(q, t)
                    final(q, t, p - 1, None).start()

    total = jnp.zeros((F, 2 * rows), F32)
    for t in range(T):
        total = total + dot(arrow[t], f_split[t], ((1,), (1,)))
    part[...] = total
    gath_sp[p] = total
    for d in range(1, n_sp):
        remote(part, gath_sp.at[p], as_sem.at[d - 1], ar_sem.at[p], {"space": lax.rem(p + d, n_sp)}).start()

    pl.when(chip < chips // 2)(early)
    join_maps(b_scan, 1)

    own_cols = pl.ds(pl.multiple_of(p * width, width), width)
    for t in range(T):
        block = diag[t, :, own_cols]
        full = folded(dot(f_split[t], block, ((1,), (0,))))
        arrow_full = dot(arrow[t], block, ((1,), (0,)))
        for n in range(nsub):
            g_loc[t, n, :rows] = full[:, cols(n)]
            g_loc[t, n, rows:] = arrow_full[:, cols(n)]

    for d in range(1, n_sp):
        come = lax.rem(p + d, n_sp)
        remote(part, gath_sp.at[come], as_sem.at[d - 1], ar_sem.at[come], {"space": come}).wait_recv()
    total = gath_sp[0]
    for i in range(1, n_sp):
        total = total + gath_sp[i]
    mine_tm[...] = total
    gath_tm[s] = total
    for d in range(1, n_tm):
        remote(mine_tm, gath_tm.at[s], ts_sem.at[d - 1], tr_sem.at[s], {"tm": lax.rem(s + d, n_tm)}).start()

    for q in range(1, n_sp):

        @pl.when(p < q)
        def _():
            remote(v_send.at[0], v_recv.at[q - 1], vs_sem.at[0], vr_sem.at[q - 1], {"space": q}).wait_recv()
            for t in range(T):
                for n in range(nsub):
                    g_loc[t, n, rows:] += v_recv[q - 1, t, n]

    def take(t, slot, parts):
        for h in parts:
            final(0, t, slot, h).wait_recv()
        for n in range(nsub):
            g_loc[t, n, :rows] += w_recv[slot, t, n]

    for t in down:
        if merging:

            @pl.when(p == 0)
            def _():
                take(t, 0, (0, 1))
                take(t, 1, (0, 1))

            @pl.when(jnp.logical_or(p == 1, p == 2))
            def _():
                take(t, 0, (None,))

        else:
            for q in range(1, n_sp):
                pl.when(p < q)(functools.partial(take, t, q - 1, (None,)))

        for n in range(nsub):
            new = g_loc[t, n]
            if t < T - 1:
                old = g_loc[t + 1, n]
                new = select(t, new - couple(old, bc[t, cols(n), :]), old)
            else:
                new = select(t, new, jnp.zeros_like(new))
            g_loc[t, n] = new

    off_copy(b_scan, g_loc.at[0]).start()
    join_offsets(b_scan, g_loc.at[0], 1)
    chain(b_scan, b_first, b_last, b_to, 1)

    for d in range(1, n_tm):
        come = lax.rem(s + d, n_tm)
        remote(mine_tm, gath_tm.at[come], ts_sem.at[d - 1], tr_sem.at[come], {"tm": come}).wait_recv()
    total = gath_tm[0]
    for i in range(1, n_tm):
        total = total + gath_tm[i]
    exact = functools.partial(
        lax.dot_general, preferred_element_type=F32, precision=lax.Precision.HIGHEST
    )
    side = tip_side[...] - total[:, :rows]
    tip_state = exact(tip_inv[...], side, (((1,), (0,)), ((), ())))
    turned = exact(tip_inv[...].T, tip_state, (((1,), (0,)), ((), ())))
    tip_out[...] = turned
    tip = turned.T

    for n in range(nsub):
        states = apply_map(b_scan["into"][n], bmap_h[n], bmap_l[n])
        for t in range(T):
            state = g_loc[t, n] + states[:, cols(t)]
            value = state[:rows] - exact(tip, state[rows:], (((1,), (0,)), ((), ())))
            sol[t, :, cols(n)] = select(t, value, jnp.zeros_like(value))

    scan_end(f_scan, driven.at[T - 1], f_last, f_to)
    scan_end(b_scan, g_loc.at[0], b_last, b_to)
    for q in range(n_sp - 1):

        @pl.when(p > q)
        def _():
            remote(v_send.at[q], v_recv.at[p - 1], vs_sem.at[q], vr_sem.at[p - 1], {"space": q}).wait_send()
            if not merging:
                for t in down:
                    final(q, t, p - 1, None).wait_send()

    if merging:

        @pl.when(p == 3)
        def _():
            for t in down:
                passing(0, t, 2, 0).wait_send()
                passing(0, t, 1, 1).wait_send()
                final(2, t, 0, None).wait_send()
                final(1, t, 0, None).wait_send()

        @pl.when(p == 2)
        def _():
            for t in down:
                passing(1, t, 3, None).wait_send()
                final(0, t, 1, 0).wait_send()
                final(0, t, 1, 1).wait_send()

        @pl.when(p == 1)
        def _():
            for t in down:
                final(0, t, 0, 0).wait_send()
                final(0, t, 0, 1).wait_send()

    for d in range(1, n_sp):
        remote(part, gath_sp.at[p], as_sem.at[d - 1], ar_sem.at[p], {"space": lax.rem(p + d, n_sp)}).wait_send()
    for d in range(1, n_tm):
        remote(mine_tm, gath_tm.at[s], ts_sem.at[d - 1], tr_sem.at[s], {"tm": lax.rem(s + d, n_tm)}).wait_send()


def scan_scratch(nsub, rows, sub):
    half = nsub // 2 if nsub % 2 == 0 else nsub
    return {
        "map": pltpu.VMEM((nsub, sub, sub), F32),
        "mate_map": pltpu.VMEM((half, sub, sub), F32),
        "two": pltpu.VMEM((half, sub, sub), F32),
        "join_h": pltpu.VMEM((half, sub, 2 * sub), BF16),
        "join_l": pltpu.VMEM((half, sub, 2 * sub), BF16),
        "mate_off": pltpu.VMEM((half, rows, sub), F32),
        "join_off": pltpu.VMEM((half, rows, 2 * sub), F32),
        "arrived": pltpu.VMEM((half, rows, sub), F32),
        "out": pltpu.VMEM((half, rows, sub), F32),
        "hand": pltpu.VMEM((half, rows, sub), F32),
        "into": pltpu.VMEM((nsub, rows, sub), F32),
        "sem": pltpu.SemaphoreType.DMA((2, 2 + 2 * half)),
    }


def on_device(n_tm, n_sp, sections, right_side, tip_side, diag_inverse, fwd, bwd, arrow_rows, tip_inverse):
    T, rows, total_width = right_side.shape
    width, sub = fwd.shape[1], fwd.shape[2]
    nsub = width // sub
    F = arrow_rows.shape[1]
    both = rows + F
    vmem = pl.BlockSpec(memory_space=pltpu.VMEM)
    maps = pltpu.VMEM((nsub, sub, T * sub), BF16)
    dma = pltpu.SemaphoreType.DMA
    others = n_sp - 1
    states, turned = pl.pallas_call(
        functools.partial(kernel, n_tm, n_sp),
        out_shape=(
            jax.ShapeDtypeStruct((T, rows, width), F32),
            jax.ShapeDtypeStruct(tip_side.shape[::-1], F32),
        ),
        in_specs=[
            pl.BlockSpec(memory_space=pltpu.SMEM),
            vmem,
            vmem,
            pl.BlockSpec(memory_space=pl.ANY),
            vmem,
            vmem,
            vmem,
            vmem,
        ],
        out_specs=(vmem, vmem),
        scratch_shapes=[
            pltpu.VMEM(diag_inverse.shape, BF16),
            maps,
            maps,
            maps,
            maps,
            pltpu.VMEM((T, nsub, rows, sub), F32),
            pltpu.VMEM((T, 2 * rows, width), BF16),
            pltpu.VMEM((T, nsub, both, sub), F32),
            pltpu.VMEM((others, T, nsub, rows, sub), F32),
            pltpu.VMEM((others, T, nsub, rows, sub), F32),
            pltpu.VMEM((T, nsub, rows, sub), F32),
            pltpu.VMEM((others, T, nsub, F, sub), F32),
            pltpu.VMEM((others, T, nsub, F, sub), F32),
            pltpu.VMEM((F, 2 * rows), F32),
            pltpu.VMEM((n_sp, F, 2 * rows), F32),
            pltpu.VMEM((n_tm, F, 2 * rows), F32),
            pltpu.VMEM((F, 2 * rows), F32),
            scan_scratch(nsub, rows, sub),
            scan_scratch(nsub, both, sub),
            dma((T,)),
            dma((others, T, 2)),
            dma((others, T, 2)),
            dma((T, 2)),
            dma((T,)),
            dma((others,)),
            dma((others,)),
            dma((others,)),
            dma((n_sp,)),
            dma((n_tm - 1,)),
            dma((n_tm,)),
        ],
        compiler_params=pltpu.CompilerParams(
            collective_id=0, has_side_effects=True, vmem_limit_bytes=56 * 1024 * 1024
        ),
        cost_estimate=pl.CostEstimate(
            flops=8 * T * rows * width * total_width, bytes_accessed=2 * diag_inverse.size, transcendentals=0
        ),
    )(sections, right_side, tip_side.T, diag_inverse, fwd, bwd, arrow_rows, tip_inverse)
    return states, turned.T


def solution(mesh):
    placed = (
        P(),
        P("tm", None, None),
        P(),
        P("tm", "space", None),
        P("tm", "space", None),
        P("tm", "space", None),
        P("tm", None, "space"),
        P(),
    )
    return jax.shard_map(
        functools.partial(on_device, mesh.shape["tm"], mesh.shape["space"]),
        mesh=mesh,
        in_specs=placed,
        out_specs=(P("tm", None, "space"), P()),
        check_vma=False,
    )
```

```python
import functools

import jax
import jax.numpy as jnp
from jax import lax
from jax.experimental import pallas as pl
from jax.experimental.pallas import tpu as pltpu
from jax.sharding import PartitionSpec as P

F32 = jnp.float32
BF16 = jnp.bfloat16
MESH = pl.DeviceIdType.MESH


def dot(a, b, contract):
    return lax.dot_general(a, b, (contract, ((), ())), preferred_element_type=F32)


def stacked(x):
    high = x.astype(BF16).astype(F32)
    return jnp.concatenate([high, x - high], 0).astype(BF16)


def folded(y):
    rows = y.shape[0] // 2
    return y[:rows] + y[rows:]


def couple(x, block):
    return folded(dot(stacked(x), block, ((1,), (1,))))


def apply_map(x, high, low):
    rows = x.shape[0]
    pieces = stacked(x)
    return folded(dot(pieces, high, ((1,), (0,)))) + dot(pieces[:rows], low, ((1,), (0,)))


def kernel(
    n_tm, n_sp, sec, rs, tip_side, diag_hbm, fc, bc, arrow, tip_inv,
    sol, tip_out,
    diag, fmap_h, fmap_l, bmap_h, bmap_l, driven, f_split, g_loc,
    w_send, w_recv, w_pass, v_send, v_recv, v_own, part, gath_sp, gath_tm, mine_tm,
    f_scan, b_scan,
    diag_sem, ws_sem, wr_sem, ps_sem, pr_sem, vs_sem, vr_sem, as_sem, ar_sem, ts_sem, tr_sem,
):
    T, rows = rs.shape[0], rs.shape[1]
    width, sub = fc.shape[1], fc.shape[2]
    nsub = width // sub
    F = arrow.shape[1]
    s, p = lax.axis_index("tm"), lax.axis_index("space")
    core, chip, chips = lax.rem(s, 2), s // 2, n_tm // 2
    length = sec[s]
    half, split = (nsub // 2, True) if nsub % 2 == 0 else (nsub, False)
    base = core * half if split else 0
    other_base = half - core * half if split else 0
    mate = s + 1 - 2 * core

    loads = [
        pltpu.make_async_copy(diag_hbm.at[t], diag.at[t], diag_sem.at[t]) for t in range(T)
    ]
    for load in loads:
        load.start()

    barrier = pltpu.get_barrier_semaphore()
    for d in range(1, n_tm):
        pl.semaphore_signal(barrier, inc=1, device_id={"tm": lax.rem(s + d, n_tm)}, device_id_type=MESH)
    for d in range(1, n_sp):
        pl.semaphore_signal(barrier, inc=1, device_id={"space": lax.rem(p + d, n_sp)}, device_id_type=MESH)

    def cols(n):
        return slice(n * sub, (n + 1) * sub)

    def select(t, new, old):
        if t == 0:
            return new
        return jnp.where(jnp.full(new.shape, length, jnp.int32) > t, new, old)

    def remote(src, dst, send, recv, to):
        return pltpu.make_async_remote_copy(
            src_ref=src, dst_ref=dst, send_sem=send, recv_sem=recv, device_id=to, device_id_type=MESH
        )

    def section_maps(jobs):
        row = lax.broadcasted_iota(jnp.int32, (sub, sub), 0)
        col = lax.broadcasted_iota(jnp.int32, (sub, sub), 1)
        eye = jnp.where(row == col, 1.0, 0.0).astype(F32)
        maps = [[eye] * nsub for _ in jobs]
        for i in range(T):
            for own, (coupling, order, high_ref, low_ref, _) in zip(maps, jobs):
                t = order[i]
                for n in range(nsub):
                    own[n] = select(t, -couple(own[n], coupling[t, cols(n), :]), own[n])
                    high = own[n].astype(BF16)
                    high_ref[n, :, cols(t)] = high
                    low_ref[n, :, cols(t)] = (own[n] - high.astype(F32)).astype(BF16)
        for own, job in zip(maps, jobs):
            for n in range(nsub):
                job[4][n] = own[n]

    def in_order(mine, theirs, lead):
        ahead = jnp.full(mine.shape, core, jnp.int32) == lead
        return jnp.where(ahead, mine, theirs), jnp.where(ahead, theirs, mine)

    def map_copy(scan):
        return remote(
            scan["map"].at[pl.ds(other_base, half)], scan["mate_map"],
            scan["sem"].at[0, 0], scan["sem"].at[1, 0], {"tm": mate},
        )

    def off_copy(scan, own):
        return remote(
            own.at[pl.ds(other_base, half)], scan["mate_off"],
            scan["sem"].at[0, 1], scan["sem"].at[1, 1], {"tm": mate},
        )

    def join_maps(scan, lead):
        map_copy(scan).wait_recv()
        for j in range(half):
            one, two = in_order(scan["map"][base + j], scan["mate_map"][j], lead)
            high = two.astype(BF16)
            both = apply_map(one, high, (two - high.astype(F32)).astype(BF16))
            for i, value in enumerate((both, one)):
                high = value.astype(BF16)
                scan["join_h"][j, :, cols(i)] = high
                scan["join_l"][j, :, cols(i)] = (value - high.astype(F32)).astype(BF16)
            scan["two"][j] = two

    def join_offsets(scan, own, lead):
        off_copy(scan, own).wait_recv()
        for j in range(half):
            one, two = in_order(own[base + j], scan["mate_off"][j], lead)
            after = scan["two"][j]
            high = after.astype(BF16)
            scan["join_off"][j, :, cols(0)] = two + apply_map(one, high, (after - high.astype(F32)).astype(BF16))
            scan["join_off"][j, :, cols(1)] = one

    def hop_copy(scan, j, to):
        return remote(
            scan["out"].at[j], scan["arrived"].at[j],
            scan["sem"].at[0, 2 + j], scan["sem"].at[1, 2 + j], {"tm": to},
        )

    def hand_copy(scan, j, at):
        return remote(
            scan["hand"].at[j], scan["into"].at[at + j],
            scan["sem"].at[0, 2 + half + j], scan["sem"].at[1, 2 + half + j], {"tm": mate},
        )

    def chain(scan, first, last, to, lead):
        def give(j, value):
            scan["out"][j] = value
            hop_copy(scan, j, to).start()

        @pl.when(first)
        def _():
            scan["arrived"][...] = jnp.zeros(scan["arrived"].shape, F32)
            for j in range(half):
                give(j, scan["join_off"][j, :, cols(0)])

        @pl.when(jnp.logical_not(first))
        def _():
            for j in range(half):
                hop_copy(scan, j, to).wait_recv()

                @pl.when(jnp.logical_not(last))
                def _():
                    after = apply_map(scan["arrived"][j], scan["join_h"][j, :, cols(0)], scan["join_l"][j, :, cols(0)])
                    give(j, scan["join_off"][j, :, cols(0)] + after)

        for j in range(half):
            arrived = scan["arrived"][j]
            after = apply_map(arrived, scan["join_h"][j, :, cols(1)], scan["join_l"][j, :, cols(1)])
            mine, theirs = in_order(arrived, scan["join_off"][j, :, cols(1)] + after, lead)
            if split:
                scan["hand"][j] = theirs
                hand_copy(scan, j, base).start()
            scan["into"][base + j] = mine
        if split:
            for j in range(half):
                hand_copy(scan, j, other_base).wait_recv()

    def scan_end(scan, own, last, to):
        map_copy(scan).wait_send()
        off_copy(scan, own).wait_send()
        for j in range(half):
            pl.when(jnp.logical_not(last))(hop_copy(scan, j, to).wait_send)
            if split:
                hand_copy(scan, j, base).wait_send()

    f_first, f_last, f_to = chip == 0, chip == chips - 1, lax.rem(s + 2, n_tm)
    b_first, b_last, b_to = f_last, f_first, lax.rem(s + n_tm - 2, n_tm)

    up, down = list(range(T)), list(range(T - 1, -1, -1))
    section_maps(((fc, up, fmap_h, fmap_l, f_scan["map"]), (bc, down, bmap_h, bmap_l, b_scan["map"])))
    carry = [None] * nsub
    for t in range(T):
        loads[t].wait()
        full = dot(rs[t], diag[t], ((1,), (1,)))
        for n in range(nsub):
            new = full[:, cols(n)]
            if t > 0:
                new = select(t, new - couple(carry[n], fc[t, cols(n), :]), carry[n])
            carry[n] = new
            driven[t, n] = new
    pl.semaphore_wait(barrier, n_tm - 1 + n_sp - 1)
    map_copy(f_scan).start()
    off_copy(f_scan, driven.at[T - 1]).start()
    map_copy(b_scan).start()
    join_maps(f_scan, 0)
    join_offsets(f_scan, driven.at[T - 1], 0)

    def early():
        for q in range(n_sp - 1):

            @pl.when(p > q)
            def _():
                for t in range(T):
                    full = dot(arrow[t], diag[t, :, q * width : (q + 1) * width], ((1,), (0,)))
                    for n in range(nsub):
                        v_send[q, t, n] = full[:, cols(n)]
                remote(v_send.at[q], v_recv.at[p - 1], vs_sem.at[q], vr_sem.at[p - 1], {"space": q}).start()

    pl.when(chip >= chips // 2)(early)

    chain(f_scan, f_first, f_last, f_to, 0)

    merging = n_sp == 4 and nsub % 2 == 0
    mid = nsub // 2

    def product(q, t):
        full = folded(dot(f_split[t], diag[t, :, q * width : (q + 1) * width], ((1,), (0,))))
        for n in range(nsub):
            w_send[q, t, n] = full[:, cols(n)]

    def piece(h):
        return pl.ds(0, nsub) if h is None else pl.ds(h * mid, mid)

    def final(q, t, slot, h):
        sem = h or 0
        return remote(
            w_send.at[q, t, piece(h)], w_recv.at[slot, t, piece(h)],
            ws_sem.at[q, t, sem], wr_sem.at[slot, t, sem], {"space": q},
        )

    def passing(q, t, to, h):
        return remote(
            w_send.at[q, t, piece(h)], w_pass.at[t, piece(h)],
            ps_sem.at[t, h or 0], pr_sem.at[t], {"space": to},
        )

    def merge(q, t, h):
        passing(q, t, 0, h).wait_recv()
        for n in range(nsub) if h is None else range(h * mid, h * mid + mid):
            w_send[q, t, n] += w_pass[t, n]

    for t in down:
        for n in range(nsub):
            state = driven[t, n] + apply_map(f_scan["into"][n], fmap_h[n, :, cols(t)], fmap_l[n, :, cols(t)])
            state = select(t, state, jnp.zeros_like(state))
            f_split[t, :, cols(n)] = stacked(state)

        if merging:

            @pl.when(p == 3)
            def _():
                product(0, t)
                passing(0, t, 2, 0).start()
                passing(0, t, 1, 1).start()

            @pl.when(p == 2)
            def _():
                product(1, t)
                passing(1, t, 3, None).start()
                product(0, t)
                final(0, t, 1, 1).start()

            @pl.when(p == 1)
            def _():
                product(0, t)
                final(0, t, 0, 0).start()

        else:
            for q in range(n_sp - 1):

                @pl.when(p > q)
                def _():
                    product(q, t)
                    final(q, t, p - 1, None).start()

    if merging:

        @pl.when(p == 3)
        def _():
            for t in down:
                product(2, t)
                final(2, t, 0, None).start()
                product(1, t)
                merge(1, t, None)
                final(1, t, 0, None).start()

        @pl.when(p == 2)
        def _():
            for t in down:
                merge(0, t, 0)
                final(0, t, 1, 0).start()

        @pl.when(p == 1)
        def _():
            for t in down:
                merge(0, t, 1)
                final(0, t, 0, 1).start()

    total = jnp.zeros((F, 2 * rows), F32)
    for t in range(T):
        total = total + dot(arrow[t], f_split[t], ((1,), (1,)))
    part[...] = total
    gath_sp[p] = total
    for d in range(1, n_sp):
        remote(part, gath_sp.at[p], as_sem.at[d - 1], ar_sem.at[p], {"space": lax.rem(p + d, n_sp)}).start()

    pl.when(chip < chips // 2)(early)
    join_maps(b_scan, 1)

    own_cols = pl.ds(pl.multiple_of(p * width, width), width)
    for t in range(T):
        block = diag[t, :, own_cols]
        full = folded(dot(f_split[t], block, ((1,), (0,))))
        arrow_full = dot(arrow[t], block, ((1,), (0,)))
        for n in range(nsub):
            g_loc[t, n] = full[:, cols(n)]
            v_own[t, n] = arrow_full[:, cols(n)]

    for d in range(1, n_sp):
        come = lax.rem(p + d, n_sp)
        remote(part, gath_sp.at[come], as_sem.at[d - 1], ar_sem.at[come], {"space": come}).wait_recv()
    total = gath_sp[0]
    for i in range(1, n_sp):
        total = total + gath_sp[i]
    mine_tm[...] = total
    gath_tm[s] = total
    for d in range(1, n_tm):
        remote(mine_tm, gath_tm.at[s], ts_sem.at[d - 1], tr_sem.at[s], {"tm": lax.rem(s + d, n_tm)}).start()

    for q in range(1, n_sp):

        @pl.when(p < q)
        def _():
            remote(v_send.at[0], v_recv.at[q - 1], vs_sem.at[0], vr_sem.at[q - 1], {"space": q}).wait_recv()
            for t in range(T):
                for n in range(nsub):
                    v_own[t, n] += v_recv[q - 1, t, n]

    for d in range(1, n_tm):
        come = lax.rem(s + d, n_tm)
        remote(mine_tm, gath_tm.at[come], ts_sem.at[d - 1], tr_sem.at[come], {"tm": come}).wait_recv()
    total = gath_tm[0]
    for i in range(1, n_tm):
        total = total + gath_tm[i]
    exact = functools.partial(
        lax.dot_general, preferred_element_type=F32, precision=lax.Precision.HIGHEST
    )
    side = tip_side[...] - total[:, :rows]
    tip_state = exact(tip_inv[...], side, (((1,), (0,)), ((), ())))
    turned = exact(tip_inv[...].T, tip_state, (((1,), (0,)), ((), ())))
    tip_out[...] = turned
    tip = turned.T

    for t in range(T):
        for n in range(nsub):
            g_loc[t, n] -= exact(tip, v_own[t, n], (((1,), (0,)), ((), ())))

    def take(t, slot, parts):
        for h in parts:
            final(0, t, slot, h).wait_recv()
        for n in range(nsub):
            g_loc[t, n] += w_recv[slot, t, n]

    for t in down:
        if merging:

            @pl.when(p == 0)
            def _():
                take(t, 0, (0, 1))
                take(t, 1, (0, 1))

            @pl.when(jnp.logical_or(p == 1, p == 2))
            def _():
                take(t, 0, (None,))

        else:
            for q in range(1, n_sp):
                pl.when(p < q)(functools.partial(take, t, q - 1, (None,)))

        for n in range(nsub):
            new = g_loc[t, n]
            if t < T - 1:
                old = g_loc[t + 1, n]
                new = select(t, new - couple(old, bc[t, cols(n), :]), old)
            else:
                new = select(t, new, jnp.zeros_like(new))
            g_loc[t, n] = new

    off_copy(b_scan, g_loc.at[0]).start()
    join_offsets(b_scan, g_loc.at[0], 1)
    chain(b_scan, b_first, b_last, b_to, 1)

    for n in range(nsub):
        states = apply_map(b_scan["into"][n], bmap_h[n], bmap_l[n])
        for t in range(T):
            sol[t, :, cols(n)] = g_loc[t, n] + states[:, cols(t)]

    scan_end(f_scan, driven.at[T - 1], f_last, f_to)
    scan_end(b_scan, g_loc.at[0], b_last, b_to)
    for q in range(n_sp - 1):

        @pl.when(p > q)
        def _():
            remote(v_send.at[q], v_recv.at[p - 1], vs_sem.at[q], vr_sem.at[p - 1], {"space": q}).wait_send()
            if not merging:
                for t in down:
                    final(q, t, p - 1, None).wait_send()

    if merging:

        @pl.when(p == 3)
        def _():
            for t in down:
                passing(0, t, 2, 0).wait_send()
                passing(0, t, 1, 1).wait_send()
                final(2, t, 0, None).wait_send()
                final(1, t, 0, None).wait_send()

        @pl.when(p == 2)
        def _():
            for t in down:
                passing(1, t, 3, None).wait_send()
                final(0, t, 1, 0).wait_send()
                final(0, t, 1, 1).wait_send()

        @pl.when(p == 1)
        def _():
            for t in down:
                final(0, t, 0, 0).wait_send()
                final(0, t, 0, 1).wait_send()

    for d in range(1, n_sp):
        remote(part, gath_sp.at[p], as_sem.at[d - 1], ar_sem.at[p], {"space": lax.rem(p + d, n_sp)}).wait_send()
    for d in range(1, n_tm):
        remote(mine_tm, gath_tm.at[s], ts_sem.at[d - 1], tr_sem.at[s], {"tm": lax.rem(s + d, n_tm)}).wait_send()


def finish(sec, states, turned, sol, tip):
    length = sec[lax.axis_index("tm")]
    for t in range(states.shape[0]):
        live = jnp.full(states.shape[1:], length, jnp.int32) > t
        sol[t] = jnp.where(live, states[t], jnp.zeros_like(states[t]))
    tip[...] = turned[...]


def scan_scratch(nsub, rows, sub):
    half = nsub // 2 if nsub % 2 == 0 else nsub
    return {
        "map": pltpu.VMEM((nsub, sub, sub), F32),
        "mate_map": pltpu.VMEM((half, sub, sub), F32),
        "two": pltpu.VMEM((half, sub, sub), F32),
        "join_h": pltpu.VMEM((half, sub, 2 * sub), BF16),
        "join_l": pltpu.VMEM((half, sub, 2 * sub), BF16),
        "mate_off": pltpu.VMEM((half, rows, sub), F32),
        "join_off": pltpu.VMEM((half, rows, 2 * sub), F32),
        "arrived": pltpu.VMEM((half, rows, sub), F32),
        "out": pltpu.VMEM((half, rows, sub), F32),
        "hand": pltpu.VMEM((half, rows, sub), F32),
        "into": pltpu.VMEM((nsub, rows, sub), F32),
        "sem": pltpu.SemaphoreType.DMA((2, 2 + 2 * half)),
    }


def on_device(n_tm, n_sp, sections, right_side, tip_side, diag_inverse, fwd, bwd, arrow_rows, tip_inverse):
    T, rows, total_width = right_side.shape
    width, sub = fwd.shape[1], fwd.shape[2]
    nsub = width // sub
    F = arrow_rows.shape[1]
    vmem = pl.BlockSpec(memory_space=pltpu.VMEM)
    maps = pltpu.VMEM((nsub, sub, T * sub), BF16)
    dma = pltpu.SemaphoreType.DMA
    others = n_sp - 1
    states, turned = pl.pallas_call(
        functools.partial(kernel, n_tm, n_sp),
        out_shape=(
            jax.ShapeDtypeStruct((T, rows, width), F32),
            jax.ShapeDtypeStruct(tip_side.shape[::-1], F32),
        ),
        in_specs=[
            pl.BlockSpec(memory_space=pltpu.SMEM),
            vmem,
            vmem,
            pl.BlockSpec(memory_space=pl.ANY),
            vmem,
            vmem,
            vmem,
            vmem,
        ],
        out_specs=(vmem, vmem),
        scratch_shapes=[
            pltpu.VMEM(diag_inverse.shape, BF16),
            maps,
            maps,
            maps,
            maps,
            pltpu.VMEM((T, nsub, rows, sub), F32),
            pltpu.VMEM((T, 2 * rows, width), BF16),
            pltpu.VMEM((T, nsub, rows, sub), F32),
            pltpu.VMEM((others, T, nsub, rows, sub), F32),
            pltpu.VMEM((others, T, nsub, rows, sub), F32),
            pltpu.VMEM((T, nsub, rows, sub), F32),
            pltpu.VMEM((others, T, nsub, F, sub), F32),
            pltpu.VMEM((others, T, nsub, F, sub), F32),
            pltpu.VMEM((T, nsub, F, sub), F32),
            pltpu.VMEM((F, 2 * rows), F32),
            pltpu.VMEM((n_sp, F, 2 * rows), F32),
            pltpu.VMEM((n_tm, F, 2 * rows), F32),
            pltpu.VMEM((F, 2 * rows), F32),
            scan_scratch(nsub, rows, sub),
            scan_scratch(nsub, rows, sub),
            dma((T,)),
            dma((others, T, 2)),
            dma((others, T, 2)),
            dma((T, 2)),
            dma((T,)),
            dma((others,)),
            dma((others,)),
            dma((others,)),
            dma((n_sp,)),
            dma((n_tm - 1,)),
            dma((n_tm,)),
        ],
        compiler_params=pltpu.CompilerParams(
            collective_id=0, has_side_effects=True, vmem_limit_bytes=56 * 1024 * 1024
        ),
        cost_estimate=pl.CostEstimate(
            flops=8 * T * rows * width * total_width, bytes_accessed=2 * diag_inverse.size, transcendentals=0
        ),
    )(sections, right_side, tip_side.T, diag_inverse, fwd, bwd, arrow_rows, tip_inverse)
    states, turned = pl.pallas_call(
        finish,
        out_shape=(
            jax.ShapeDtypeStruct(states.shape, F32),
            jax.ShapeDtypeStruct(turned.shape, F32),
        ),
        in_specs=[pl.BlockSpec(memory_space=pltpu.SMEM), vmem, vmem],
        out_specs=(vmem, vmem),
    )(sections, states, turned)
    return states, turned.T


def solution(mesh):
    placed = (
        P(),
        P("tm", None, None),
        P(),
        P("tm", "space", None),
        P("tm", "space", None),
        P("tm", "space", None),
        P("tm", None, "space"),
        P(),
    )
    return jax.shard_map(
        functools.partial(on_device, mesh.shape["tm"], mesh.shape["space"]),
        mesh=mesh,
        in_specs=placed,
        out_specs=(P("tm", None, "space"), P()),
        check_vma=False,
    )
```

```python
import functools

import jax
import jax.numpy as jnp
from jax import lax
from jax.experimental import pallas as pl
from jax.experimental.pallas import tpu as pltpu
from jax.sharding import PartitionSpec as P

F32 = jnp.float32
BF16 = jnp.bfloat16
MESH = pl.DeviceIdType.MESH


def dot(a, b, contract):
    return lax.dot_general(a, b, (contract, ((), ())), preferred_element_type=F32)


def stacked(x):
    high = x.astype(BF16).astype(F32)
    return jnp.concatenate([high, x - high], 0).astype(BF16)


def folded(y):
    rows = y.shape[0] // 2
    return y[:rows] + y[rows:]


def couple(x, block):
    return folded(dot(stacked(x), block, ((1,), (1,))))


def halves(x):
    high = x.astype(BF16)
    return high, (x - high.astype(F32)).astype(BF16)


def apply_map(x, high, low):
    rows = x.shape[0]
    pieces = stacked(x)
    return folded(dot(pieces, high, ((1,), (1,)))) + dot(pieces[:rows], low, ((1,), (1,)))


def product_of(x, y):
    high, low = halves(y)
    rows = x.shape[0]
    pieces = stacked(x)
    return folded(dot(pieces, high, ((1,), (0,)))) + dot(pieces[:rows], low, ((1,), (0,)))


def kernel(
    n_tm, n_sp, sec, rs_hbm, tip_side, diag_hbm, fc_hbm, bc_hbm, arrow, tip_inv,
    sol, tip_out,
    rs, fc, bc, diag, fmap_h, fmap_l, bmap_h, bmap_l, driven, f_split, g_loc,
    w_send, w_recv, w_pass, v_send, v_recv, v_own, part, gath_sp, gath_tm, mine_tm,
    f_scan, b_scan,
    in_sem, diag_sem, ws_sem, wr_sem, ps_sem, pr_sem, vs_sem, vr_sem, as_sem, ar_sem, ts_sem, tr_sem,
):
    T, rows = rs_hbm.shape[0], rs_hbm.shape[1]
    width, sub = fc_hbm.shape[1], fc_hbm.shape[2]
    nsub = width // sub
    F = arrow.shape[1]
    s, p = lax.axis_index("tm"), lax.axis_index("space")
    core, chip, chips = lax.rem(s, 2), s // 2, n_tm // 2
    length = sec[s]
    half, split = (nsub // 2, True) if nsub % 2 == 0 else (nsub, False)
    base = core * half if split else 0
    other_base = half - core * half if split else 0
    mate = s + 1 - 2 * core

    first_loads = [
        pltpu.make_async_copy(src, dst, in_sem.at[i])
        for i, (src, dst) in enumerate(((fc_hbm, fc), (rs_hbm, rs), (bc_hbm, bc)))
    ]
    loads = [
        pltpu.make_async_copy(diag_hbm.at[t], diag.at[t], diag_sem.at[t]) for t in range(T)
    ]
    for load in first_loads[:2] + loads + first_loads[2:]:
        load.start()

    barrier = pltpu.get_barrier_semaphore()
    for d in range(1, n_tm):
        pl.semaphore_signal(barrier, inc=1, device_id={"tm": lax.rem(s + d, n_tm)}, device_id_type=MESH)
    for d in range(1, n_sp):
        pl.semaphore_signal(barrier, inc=1, device_id={"space": lax.rem(p + d, n_sp)}, device_id_type=MESH)

    def cols(n):
        return slice(n * sub, (n + 1) * sub)

    def select(t, new, old):
        if t == 0:
            return new
        return jnp.where(jnp.full(new.shape, length, jnp.int32) > t, new, old)

    def remote(src, dst, send, recv, to):
        return pltpu.make_async_remote_copy(
            src_ref=src, dst_ref=dst, send_sem=send, recv_sem=recv, device_id=to, device_id_type=MESH
        )

    def section_maps(coupling, order, high_ref, low_ref, own_map):
        row = lax.broadcasted_iota(jnp.int32, (sub, sub), 0)
        col = lax.broadcasted_iota(jnp.int32, (sub, sub), 1)
        maps = [jnp.where(row == col, 1.0, 0.0).astype(F32)] * nsub
        for i, t in enumerate(order):
            for n in range(nsub):
                block = coupling[t, cols(n), :]
                if i == 0:
                    new = -block.astype(F32)
                else:
                    both = dot(block, jnp.concatenate(halves(maps[n]), 1), ((1,), (0,)))
                    new = -(both[:, :sub] + both[:, sub:])
                maps[n] = select(t, new, maps[n])
                high_ref[n, cols(t), :], low_ref[n, cols(t), :] = halves(maps[n])
        for n in range(nsub):
            own_map[n] = maps[n]

    def in_order(mine, theirs, lead):
        ahead = jnp.full(mine.shape, core, jnp.int32) == lead
        return jnp.where(ahead, mine, theirs), jnp.where(ahead, theirs, mine)

    def map_copy(scan):
        return remote(
            scan["map"].at[pl.ds(other_base, half)], scan["mate_map"],
            scan["sem"].at[0, 0], scan["sem"].at[1, 0], {"tm": mate},
        )

    def off_copy(scan, own):
        return remote(
            own.at[pl.ds(other_base, half)], scan["mate_off"],
            scan["sem"].at[0, 1], scan["sem"].at[1, 1], {"tm": mate},
        )

    def join_maps(scan, lead):
        for j in range(half):
            one, two = in_order(scan["map"][base + j], scan["mate_map"][j], lead)
            for i, value in enumerate((product_of(two, one), one)):
                scan["join_h"][j, cols(i), :], scan["join_l"][j, cols(i), :] = halves(value)

    def join_offsets(scan, own, lead):
        off_copy(scan, own).wait_recv()
        for j in range(half):
            _, after = in_order(scan["map"][base + j], scan["mate_map"][j], lead)
            one, two = in_order(own[base + j], scan["mate_off"][j], lead)
            scan["join_off"][j, :, cols(0)] = two + apply_map(one, *halves(after))
            scan["join_off"][j, :, cols(1)] = one

    def hop_copy(scan, j, to):
        return remote(
            scan["out"].at[j], scan["arrived"].at[j],
            scan["sem"].at[0, 2 + j], scan["sem"].at[1, 2 + j], {"tm": to},
        )

    def hand_copy(scan, j, at):
        return remote(
            scan["hand"].at[j], scan["into"].at[at + j],
            scan["sem"].at[0, 2 + half + j], scan["sem"].at[1, 2 + half + j], {"tm": mate},
        )

    def give(scan, j, to, value):
        scan["out"][j] = value
        hop_copy(scan, j, to).start()

    def chain_start(scan, first, to):
        @pl.when(first)
        def _():
            scan["arrived"][...] = jnp.zeros(scan["arrived"].shape, F32)
            for j in range(half):
                give(scan, j, to, scan["join_off"][j, :, cols(0)])

    def chain(scan, first, last, to, lead):
        @pl.when(jnp.logical_not(first))
        def _():
            for j in range(half):
                hop_copy(scan, j, to).wait_recv()

                @pl.when(jnp.logical_not(last))
                def _():
                    after = apply_map(scan["arrived"][j], scan["join_h"][j, cols(0), :], scan["join_l"][j, cols(0), :])
                    give(scan, j, to, scan["join_off"][j, :, cols(0)] + after)

        for j in range(half):
            arrived = scan["arrived"][j]
            after = apply_map(arrived, scan["join_h"][j, cols(1), :], scan["join_l"][j, cols(1), :])
            mine, theirs = in_order(arrived, scan["join_off"][j, :, cols(1)] + after, lead)
            if split:
                scan["hand"][j] = theirs
                hand_copy(scan, j, base).start()
            scan["into"][base + j] = mine

    def lanes(n):
        return pl.ds(pl.multiple_of(n * sub, sub), sub)

    def scan_end(scan, own, last, to):
        map_copy(scan).wait_send()
        off_copy(scan, own).wait_send()
        for j in range(half):
            pl.when(jnp.logical_not(last))(hop_copy(scan, j, to).wait_send)
            if split:
                hand_copy(scan, j, base).wait_send()

    f_first, f_last, f_to = chip == 0, chip == chips - 1, lax.rem(s + 2, n_tm)
    b_first, b_last, b_to = f_last, f_first, lax.rem(s + n_tm - 2, n_tm)

    up, down = list(range(T)), list(range(T - 1, -1, -1))
    first_loads[0].wait()
    section_maps(fc, up, fmap_h, fmap_l, f_scan["map"])
    first_loads[1].wait()
    carry = [None] * nsub
    for t in range(T):
        loads[t].wait()
        full = dot(rs[t], diag[t], ((1,), (1,)))
        for n in range(nsub):
            new = full[:, cols(n)]
            if t > 0:
                new = select(t, new - couple(carry[n], fc[t, cols(n), :]), carry[n])
            carry[n] = new
            driven[t, n] = new
    pl.semaphore_wait(barrier, n_tm - 1 + n_sp - 1)
    map_copy(f_scan).start()
    off_copy(f_scan, driven.at[T - 1]).start()
    for load in first_loads[2:]:
        load.wait()
    section_maps(bc, down, bmap_h, bmap_l, b_scan["map"])
    map_copy(b_scan).start()
    map_copy(f_scan).wait_recv()
    join_offsets(f_scan, driven.at[T - 1], 0)
    chain_start(f_scan, f_first, f_to)
    join_maps(f_scan, 0)

    def early():
        for q in range(n_sp - 1):

            @pl.when(p > q)
            def _():
                for t in range(T):
                    full = dot(arrow[t], diag[t, :, q * width : (q + 1) * width], ((1,), (0,)))
                    for n in range(nsub):
                        v_send[q, t, n] = full[:, cols(n)]
                remote(v_send.at[q], v_recv.at[p - 1], vs_sem.at[q], vr_sem.at[p - 1], {"space": q}).start()

    pl.when(chip >= chips // 2)(early)

    chain(f_scan, f_first, f_last, f_to, 0)

    def forward_state(t, n):
        state = driven[t, n] + apply_map(f_scan["into"][n], fmap_h[n, cols(t), :], fmap_l[n, cols(t), :])
        state = select(t, state, jnp.zeros_like(state))
        f_split[t, :, lanes(n)] = stacked(state)

    if split:
        for t in down:
            for j in range(half):
                forward_state(t, base + j)
        for j in range(half):
            hand_copy(f_scan, j, other_base).wait_recv()

    merging = n_sp == 4 and nsub % 2 == 0
    mid = nsub // 2

    def product(q, t):
        full = folded(dot(f_split[t], diag[t, :, q * width : (q + 1) * width], ((1,), (0,))))
        for n in range(nsub):
            w_send[q, t, n] = full[:, cols(n)]

    def piece(h):
        return pl.ds(0, nsub) if h is None else pl.ds(h * mid, mid)

    def final(q, t, slot, h):
        sem = h or 0
        return remote(
            w_send.at[q, t, piece(h)], w_recv.at[slot, t, piece(h)],
            ws_sem.at[q, t, sem], wr_sem.at[slot, t, sem], {"space": q},
        )

    def passing(q, t, to, h):
        return remote(
            w_send.at[q, t, piece(h)], w_pass.at[t, piece(h)],
            ps_sem.at[t, h or 0], pr_sem.at[t], {"space": to},
        )

    def merge(q, t, h):
        passing(q, t, 0, h).wait_recv()
        for n in range(nsub) if h is None else range(h * mid, h * mid + mid):
            w_send[q, t, n] += w_pass[t, n]

    for t in down:
        for j in range(half):
            forward_state(t, other_base + j)

        if merging:

            @pl.when(p == 3)
            def _():
                product(0, t)
                passing(0, t, 2, 0).start()
                passing(0, t, 1, 1).start()

            @pl.when(p == 2)
            def _():
                product(1, t)
                passing(1, t, 3, None).start()
                product(0, t)
                final(0, t, 1, 1).start()

            @pl.when(p == 1)
            def _():
                product(0, t)
                final(0, t, 0, 0).start()

        else:
            for q in range(n_sp - 1):

                @pl.when(p > q)
                def _():
                    product(q, t)
                    final(q, t, p - 1, None).start()

    if merging:

        @pl.when(p == 3)
        def _():
            for t in down:
                product(2, t)
                final(2, t, 0, None).start()
                product(1, t)
                merge(1, t, None)
                final(1, t, 0, None).start()

        @pl.when(p == 2)
        def _():
            for t in down:
                merge(0, t, 0)
                final(0, t, 1, 0).start()

        @pl.when(p == 1)
        def _():
            for t in down:
                merge(0, t, 1)
                final(0, t, 0, 1).start()

    total = jnp.zeros((F, 2 * rows), F32)
    for t in range(T):
        total = total + dot(arrow[t], f_split[t], ((1,), (1,)))
    part[...] = total
    gath_sp[p] = total
    for d in range(1, n_sp):
        remote(part, gath_sp.at[p], as_sem.at[d - 1], ar_sem.at[p], {"space": lax.rem(p + d, n_sp)}).start()

    pl.when(chip < chips // 2)(early)
    map_copy(b_scan).wait_recv()
    join_maps(b_scan, 1)

    own_cols = pl.ds(pl.multiple_of(p * width, width), width)
    for t in range(T):
        block = diag[t, :, own_cols]
        full = folded(dot(f_split[t], block, ((1,), (0,))))
        arrow_full = dot(arrow[t], block, ((1,), (0,)))
        for n in range(nsub):
            g_loc[t, n] = full[:, cols(n)]
            v_own[t, n] = arrow_full[:, cols(n)]

    for d in range(1, n_sp):
        come = lax.rem(p + d, n_sp)
        remote(part, gath_sp.at[come], as_sem.at[d - 1], ar_sem.at[come], {"space": come}).wait_recv()
    total = gath_sp[0]
    for i in range(1, n_sp):
        total = total + gath_sp[i]
    mine_tm[...] = total
    gath_tm[s] = total
    for d in range(1, n_tm):
        remote(mine_tm, gath_tm.at[s], ts_sem.at[d - 1], tr_sem.at[s], {"tm": lax.rem(s + d, n_tm)}).start()

    for q in range(1, n_sp):

        @pl.when(p < q)
        def _():
            remote(v_send.at[0], v_recv.at[q - 1], vs_sem.at[0], vr_sem.at[q - 1], {"space": q}).wait_recv()
            for t in range(T):
                for n in range(nsub):
                    v_own[t, n] += v_recv[q - 1, t, n]

    for d in range(1, n_tm):
        come = lax.rem(s + d, n_tm)
        remote(mine_tm, gath_tm.at[come], ts_sem.at[d - 1], tr_sem.at[come], {"tm": come}).wait_recv()
    total = gath_tm[0]
    for i in range(1, n_tm):
        total = total + gath_tm[i]
    exact = functools.partial(
        lax.dot_general, preferred_element_type=F32, precision=lax.Precision.HIGHEST
    )
    side = tip_side[...] - total[:, :rows]
    tip_state = exact(tip_inv[...], side, (((1,), (0,)), ((), ())))
    turned = exact(tip_inv[...].T, tip_state, (((1,), (0,)), ((), ())))
    tip_out[...] = turned
    tip = turned.T

    for t in range(T):
        for n in range(nsub):
            g_loc[t, n] -= exact(tip, v_own[t, n], (((1,), (0,)), ((), ())))

    def take(t, slot, parts):
        for h in parts:
            final(0, t, slot, h).wait_recv()
        for n in range(nsub):
            g_loc[t, n] += w_recv[slot, t, n]

    for t in down:
        if merging:

            @pl.when(p == 0)
            def _():
                take(t, 0, (0, 1))
                take(t, 1, (0, 1))

            @pl.when(jnp.logical_or(p == 1, p == 2))
            def _():
                take(t, 0, (None,))

        else:
            for q in range(1, n_sp):
                pl.when(p < q)(functools.partial(take, t, q - 1, (None,)))

        for n in range(nsub):
            new = g_loc[t, n]
            if t < T - 1:
                old = g_loc[t + 1, n]
                new = select(t, new - couple(old, bc[t, cols(n), :]), old)
            else:
                new = select(t, new, jnp.zeros_like(new))
            g_loc[t, n] = new

    off_copy(b_scan, g_loc.at[0]).start()
    join_offsets(b_scan, g_loc.at[0], 1)
    chain_start(b_scan, b_first, b_to)
    chain(b_scan, b_first, b_last, b_to, 1)

    def backward_states(n):
        states = apply_map(b_scan["into"][n], bmap_h[n], bmap_l[n])
        for t in range(T):
            sol[t, :, lanes(n)] = g_loc[t, n] + states[:, cols(t)]

    if split:
        for j in range(half):
            backward_states(base + j)
        for j in range(half):
            hand_copy(b_scan, j, other_base).wait_recv()
    for j in range(half):
        backward_states(other_base + j)

    scan_end(f_scan, driven.at[T - 1], f_last, f_to)
    scan_end(b_scan, g_loc.at[0], b_last, b_to)
    for q in range(n_sp - 1):

        @pl.when(p > q)
        def _():
            remote(v_send.at[q], v_recv.at[p - 1], vs_sem.at[q], vr_sem.at[p - 1], {"space": q}).wait_send()
            if not merging:
                for t in down:
                    final(q, t, p - 1, None).wait_send()

    if merging:

        @pl.when(p == 3)
        def _():
            for t in down:
                passing(0, t, 2, 0).wait_send()
                passing(0, t, 1, 1).wait_send()
                final(2, t, 0, None).wait_send()
                final(1, t, 0, None).wait_send()

        @pl.when(p == 2)
        def _():
            for t in down:
                passing(1, t, 3, None).wait_send()
                final(0, t, 1, 0).wait_send()
                final(0, t, 1, 1).wait_send()

        @pl.when(p == 1)
        def _():
            for t in down:
                final(0, t, 0, 0).wait_send()
                final(0, t, 0, 1).wait_send()

    for d in range(1, n_sp):
        remote(part, gath_sp.at[p], as_sem.at[d - 1], ar_sem.at[p], {"space": lax.rem(p + d, n_sp)}).wait_send()
    for d in range(1, n_tm):
        remote(mine_tm, gath_tm.at[s], ts_sem.at[d - 1], tr_sem.at[s], {"tm": lax.rem(s + d, n_tm)}).wait_send()


def finish(sec, states, turned, sol, tip):
    length = sec[lax.axis_index("tm")]
    for t in range(states.shape[0]):
        live = jnp.full(states.shape[1:], length, jnp.int32) > t
        sol[t] = jnp.where(live, states[t], jnp.zeros_like(states[t]))
    tip[...] = turned[...]


def scan_scratch(nsub, rows, sub):
    half = nsub // 2 if nsub % 2 == 0 else nsub
    return {
        "map": pltpu.VMEM((nsub, sub, sub), F32),
        "mate_map": pltpu.VMEM((half, sub, sub), F32),
        "join_h": pltpu.VMEM((half, 2 * sub, sub), BF16),
        "join_l": pltpu.VMEM((half, 2 * sub, sub), BF16),
        "mate_off": pltpu.VMEM((half, rows, sub), F32),
        "join_off": pltpu.VMEM((half, rows, 2 * sub), F32),
        "arrived": pltpu.VMEM((half, rows, sub), F32),
        "out": pltpu.VMEM((half, rows, sub), F32),
        "hand": pltpu.VMEM((half, rows, sub), F32),
        "into": pltpu.VMEM((nsub, rows, sub), F32),
        "sem": pltpu.SemaphoreType.DMA((2, 2 + 2 * half)),
    }


def on_device(n_tm, n_sp, sections, right_side, tip_side, diag_inverse, fwd, bwd, arrow_rows, tip_inverse):
    T, rows, total_width = right_side.shape
    width, sub = fwd.shape[1], fwd.shape[2]
    nsub = width // sub
    F = arrow_rows.shape[1]
    vmem, hbm = pl.BlockSpec(memory_space=pltpu.VMEM), pl.BlockSpec(memory_space=pl.ANY)
    maps = pltpu.VMEM((nsub, T * sub, sub), BF16)
    dma = pltpu.SemaphoreType.DMA
    others = n_sp - 1
    states, turned = pl.pallas_call(
        functools.partial(kernel, n_tm, n_sp),
        out_shape=(
            jax.ShapeDtypeStruct((T, rows, width), F32),
            jax.ShapeDtypeStruct(tip_side.shape[::-1], F32),
        ),
        in_specs=[
            pl.BlockSpec(memory_space=pltpu.SMEM),
            hbm,
            vmem,
            hbm,
            hbm,
            hbm,
            vmem,
            vmem,
        ],
        out_specs=(vmem, vmem),
        scratch_shapes=[
            pltpu.VMEM(right_side.shape, BF16),
            pltpu.VMEM(fwd.shape, BF16),
            pltpu.VMEM(bwd.shape, BF16),
            pltpu.VMEM(diag_inverse.shape, BF16),
            maps,
            maps,
            maps,
            maps,
            pltpu.VMEM((T, nsub, rows, sub), F32),
            pltpu.VMEM((T, 2 * rows, width), BF16),
            pltpu.VMEM((T, nsub, rows, sub), F32),
            pltpu.VMEM((others, T, nsub, rows, sub), F32),
            pltpu.VMEM((others, T, nsub, rows, sub), F32),
            pltpu.VMEM((T, nsub, rows, sub), F32),
            pltpu.VMEM((others, T, nsub, F, sub), F32),
            pltpu.VMEM((others, T, nsub, F, sub), F32),
            pltpu.VMEM((T, nsub, F, sub), F32),
            pltpu.VMEM((F, 2 * rows), F32),
            pltpu.VMEM((n_sp, F, 2 * rows), F32),
            pltpu.VMEM((n_tm, F, 2 * rows), F32),
            pltpu.VMEM((F, 2 * rows), F32),
            scan_scratch(nsub, rows, sub),
            scan_scratch(nsub, rows, sub),
            dma((3,)),
            dma((T,)),
            dma((others, T, 2)),
            dma((others, T, 2)),
            dma((T, 2)),
            dma((T,)),
            dma((others,)),
            dma((others,)),
            dma((others,)),
            dma((n_sp,)),
            dma((n_tm - 1,)),
            dma((n_tm,)),
        ],
        compiler_params=pltpu.CompilerParams(
            collective_id=0, has_side_effects=True, vmem_limit_bytes=56 * 1024 * 1024
        ),
        cost_estimate=pl.CostEstimate(
            flops=8 * T * rows * width * total_width, bytes_accessed=2 * diag_inverse.size, transcendentals=0
        ),
    )(sections, right_side, tip_side.T, diag_inverse, fwd, bwd, arrow_rows, tip_inverse)
    states, turned = pl.pallas_call(
        finish,
        out_shape=(
            jax.ShapeDtypeStruct(states.shape, F32),
            jax.ShapeDtypeStruct(turned.shape, F32),
        ),
        in_specs=[pl.BlockSpec(memory_space=pltpu.SMEM), vmem, vmem],
        out_specs=(vmem, vmem),
    )(sections, states, turned)
    return states, turned.T


def solution(mesh):
    placed = (
        P(),
        P("tm", None, None),
        P(),
        P("tm", "space", None),
        P("tm", "space", None),
        P("tm", "space", None),
        P("tm", None, "space"),
        P(),
    )
    return jax.shard_map(
        functools.partial(on_device, mesh.shape["tm"], mesh.shape["space"]),
        mesh=mesh,
        in_specs=placed,
        out_specs=(P("tm", None, "space"), P()),
        check_vma=False,
    )
```

```python
import functools

import jax
import jax.numpy as jnp
from jax import lax
from jax.experimental import pallas as pl
from jax.experimental.pallas import tpu as pltpu
from jax.sharding import PartitionSpec as P

F32 = jnp.float32
BF16 = jnp.bfloat16
MESH = pl.DeviceIdType.MESH


def dot(a, b, contract):
    return lax.dot_general(a, b, (contract, ((), ())), preferred_element_type=F32)


def stacked(x):
    high = x.astype(BF16).astype(F32)
    return jnp.concatenate([high, x - high], 0).astype(BF16)


def folded(y):
    rows = y.shape[0] // 2
    return y[:rows] + y[rows:]


def couple(x, block):
    return folded(dot(stacked(x), block, ((1,), (1,))))


def halves(x):
    high = x.astype(BF16)
    return high, (x - high.astype(F32)).astype(BF16)


def apply_map(x, high, low):
    rows = x.shape[0]
    pieces = stacked(x)
    return folded(dot(pieces, high, ((1,), (1,)))) + dot(pieces[:rows], low, ((1,), (1,)))


def product_of(x, y):
    high, low = halves(y)
    rows = x.shape[0]
    pieces = stacked(x)
    return folded(dot(pieces, high, ((1,), (0,)))) + dot(pieces[:rows], low, ((1,), (0,)))


def kernel(
    n_tm, n_sp, sec, rs_hbm, tip_side, diag_hbm, fc_hbm, bc_hbm, arrow, tip_inv,
    sol, tip_out,
    rs, fc, bc, diag, fmap_h, fmap_l, bmap_h, bmap_l, driven, f_split, g_loc,
    w_send, w_recv, w_pass, v_send, v_recv, v_own, part, gath_sp, gath_tm, mine_tm,
    f_scan, b_scan,
    in_sem, diag_sem, ws_sem, wr_sem, ps_sem, pr_sem, vs_sem, vr_sem, as_sem, ar_sem, ts_sem, tr_sem,
):
    T, rows = rs_hbm.shape[0], rs_hbm.shape[1]
    width, sub = fc_hbm.shape[1], fc_hbm.shape[2]
    nsub = width // sub
    F = arrow.shape[1]
    s, p = lax.axis_index("tm"), lax.axis_index("space")
    core, chip, chips = lax.rem(s, 2), s // 2, n_tm // 2
    length = sec[s]
    half, split = (nsub // 2, True) if nsub % 2 == 0 else (nsub, False)
    base = core * half if split else 0
    other_base = half - core * half if split else 0
    mate = s + 1 - 2 * core

    first_loads = [
        pltpu.make_async_copy(src, dst, in_sem.at[i])
        for i, (src, dst) in enumerate(((fc_hbm, fc), (bc_hbm, bc), (rs_hbm, rs)))
    ]
    loads = [
        pltpu.make_async_copy(diag_hbm.at[t], diag.at[t], diag_sem.at[t]) for t in range(T)
    ]
    for load in first_loads + loads:
        load.start()

    barrier = pltpu.get_barrier_semaphore()
    for d in range(1, n_tm):
        pl.semaphore_signal(barrier, inc=1, device_id={"tm": lax.rem(s + d, n_tm)}, device_id_type=MESH)
    for d in range(1, n_sp):
        pl.semaphore_signal(barrier, inc=1, device_id={"space": lax.rem(p + d, n_sp)}, device_id_type=MESH)

    def cols(n):
        return slice(n * sub, (n + 1) * sub)

    def select(t, new, old):
        if t == 0:
            return new
        return jnp.where(jnp.full(new.shape, length, jnp.int32) > t, new, old)

    def remote(src, dst, send, recv, to):
        return pltpu.make_async_remote_copy(
            src_ref=src, dst_ref=dst, send_sem=send, recv_sem=recv, device_id=to, device_id_type=MESH
        )

    def section_maps(coupling, order, high_ref, low_ref, own_map):
        row = lax.broadcasted_iota(jnp.int32, (sub, sub), 0)
        col = lax.broadcasted_iota(jnp.int32, (sub, sub), 1)
        maps = [jnp.where(row == col, 1.0, 0.0).astype(F32)] * nsub
        for i, t in enumerate(order):
            for n in range(nsub):
                block = coupling[t, cols(n), :]
                if i == 0:
                    new = -block.astype(F32)
                else:
                    both = dot(block, jnp.concatenate(halves(maps[n]), 1), ((1,), (0,)))
                    new = -(both[:, :sub] + both[:, sub:])
                maps[n] = select(t, new, maps[n])
                high_ref[n, cols(t), :], low_ref[n, cols(t), :] = halves(maps[n])
        for n in range(nsub):
            own_map[n] = maps[n]

    def in_order(mine, theirs, lead):
        ahead = jnp.full(mine.shape, core, jnp.int32) == lead
        return jnp.where(ahead, mine, theirs), jnp.where(ahead, theirs, mine)

    def map_copy(scan):
        return remote(
            scan["map"].at[pl.ds(other_base, half)], scan["mate_map"],
            scan["sem"].at[0, 0], scan["sem"].at[1, 0], {"tm": mate},
        )

    def off_copy(scan, own):
        return remote(
            own.at[pl.ds(other_base, half)], scan["mate_off"],
            scan["sem"].at[0, 1], scan["sem"].at[1, 1], {"tm": mate},
        )

    def pair_map_copy(scan, way):
        return remote(
            scan["chip_map"], scan["ahead_map"],
            scan["sem"].at[0, 2 + 2 * half], scan["sem"].at[1, 2 + 2 * half], {"tm": away(way, 2)},
        )

    def pair_off_copy(scan, j, way):
        at = 3 + 2 * half + j
        return remote(
            scan["chip_off"].at[j], scan["ahead_off"].at[j],
            scan["sem"].at[0, at], scan["sem"].at[1, at], {"tm": away(way, 2)},
        )

    def away(way, steps):
        return lax.rem(s + n_tm + way * steps, n_tm)

    def join_maps(scan, lead, first_of_pair, way):
        for j in range(half):
            one, two = in_order(scan["map"][base + j], scan["mate_map"][j], lead)
            scan["one_h"][j], scan["one_l"][j] = halves(one)
            both = product_of(two, one)
            scan["chip_map"][j] = both
            scan["chip_h"][j], scan["chip_l"][j] = halves(both)
        pl.when(first_of_pair)(pair_map_copy(scan, way).start)

    def join_offsets(scan, own, lead, first_of_pair, way):
        off_copy(scan, own).wait_recv()
        for j in range(half):
            _, after = in_order(scan["map"][base + j], scan["mate_map"][j], lead)
            one, two = in_order(own[base + j], scan["mate_off"][j], lead)
            scan["chip_off"][j] = two + apply_map(one, *halves(after))
            scan["one_off"][j] = one
            pl.when(first_of_pair)(pair_off_copy(scan, j, way).start)

    def hop_copy(scan, j, to, far):
        at = 3 + 3 * half + j if far else 2 + j
        return remote(
            scan["out"].at[j], scan["arrived"].at[j],
            scan["sem"].at[0, at], scan["sem"].at[1, 2 + j], {"tm": to},
        )

    def hand_copy(scan, j, at):
        return remote(
            scan["hand"].at[j], scan["into"].at[at + j],
            scan["sem"].at[0, 2 + half + j], scan["sem"].at[1, 2 + half + j], {"tm": mate},
        )

    def chain(scan, first, last, lead, first_of_pair, way):
        second = jnp.logical_not(first_of_pair)
        later = jnp.logical_not(first)

        @pl.when(jnp.logical_and(second, later))
        def _():
            pair_map_copy(scan, way).wait_recv()

        for j in range(half):

            @pl.when(second)
            def _():
                pair_off_copy(scan, j, way).wait_recv()
                scan["chip_in"][j] = scan["ahead_off"][j]

            @pl.when(jnp.logical_and(first_of_pair, first))
            def _():
                scan["chip_in"][j] = jnp.zeros((rows, sub), F32)

            pl.when(later)(hop_copy(scan, j, mate, False).wait_recv)

            @pl.when(jnp.logical_and(first_of_pair, later))
            def _():
                scan["chip_in"][j] = scan["arrived"][j]

            @pl.when(jnp.logical_and(second, later))
            def _():
                scan["chip_in"][j] += apply_map(scan["arrived"][j], *halves(scan["ahead_map"][j]))

            @pl.when(jnp.logical_and(second, jnp.logical_not(last)))
            def _():
                after = apply_map(scan["chip_in"][j], scan["chip_h"][j], scan["chip_l"][j])
                scan["out"][j] = scan["chip_off"][j] + after
                hop_copy(scan, j, away(way, 4), True).start()
                hop_copy(scan, j, away(way, 2), False).start()

        for j in range(half):
            chip_in = scan["chip_in"][j]
            after = apply_map(chip_in, scan["one_h"][j], scan["one_l"][j])
            mine, theirs = in_order(chip_in, scan["one_off"][j] + after, lead)
            if split:
                scan["hand"][j] = theirs
                hand_copy(scan, j, base).start()
            scan["into"][base + j] = mine

        @pl.when(jnp.logical_and(second, first))
        def _():
            pair_map_copy(scan, way).wait_recv()

    def lanes(n):
        return pl.ds(pl.multiple_of(n * sub, sub), sub)

    def scan_end(scan, own, last, first_of_pair, way):
        map_copy(scan).wait_send()
        off_copy(scan, own).wait_send()

        @pl.when(first_of_pair)
        def _():
            pair_map_copy(scan, way).wait_send()
            for j in range(half):
                pair_off_copy(scan, j, way).wait_send()

        @pl.when(jnp.logical_not(jnp.logical_or(first_of_pair, last)))
        def _():
            for j in range(half):
                hop_copy(scan, j, away(way, 4), True).wait_send()
                hop_copy(scan, j, away(way, 2), False).wait_send()

        if split:
            for j in range(half):
                hand_copy(scan, j, base).wait_send()

    f_first, f_last = chip // 2 == 0, chip // 2 == chips // 2 - 1
    b_first, b_last = f_last, f_first
    f_lead, b_lead = lax.rem(chip, 2) == 0, lax.rem(chip, 2) == 1

    up, down = list(range(T)), list(range(T - 1, -1, -1))
    first_loads[0].wait()
    section_maps(fc, up, fmap_h, fmap_l, f_scan["map"])
    first_loads[1].wait()
    section_maps(bc, down, bmap_h, bmap_l, b_scan["map"])
    first_loads[2].wait()
    carry = [None] * nsub
    for t in range(T):
        loads[t].wait()
        full = dot(rs[t], diag[t], ((1,), (1,)))
        for n in range(nsub):
            new = full[:, cols(n)]
            if t > 0:
                new = select(t, new - couple(carry[n], fc[t, cols(n), :]), carry[n])
            carry[n] = new
            driven[t, n] = new
    pl.semaphore_wait(barrier, n_tm - 1 + n_sp - 1)
    map_copy(f_scan).start()
    off_copy(f_scan, driven.at[T - 1]).start()
    map_copy(b_scan).start()
    map_copy(f_scan).wait_recv()
    join_offsets(f_scan, driven.at[T - 1], 0, f_lead, 1)
    join_maps(f_scan, 0, f_lead, 1)

    def early():
        for q in range(n_sp - 1):

            @pl.when(p > q)
            def _():
                for t in range(T):
                    full = dot(arrow[t], diag[t, :, q * width : (q + 1) * width], ((1,), (0,)))
                    for n in range(nsub):
                        v_send[q, t, n] = full[:, cols(n)]
                remote(v_send.at[q], v_recv.at[p - 1], vs_sem.at[q], vr_sem.at[p - 1], {"space": q}).start()

    pl.when(chip >= chips // 2)(early)

    chain(f_scan, f_first, f_last, 0, f_lead, 1)

    def forward_state(t, n):
        state = driven[t, n] + apply_map(f_scan["into"][n], fmap_h[n, cols(t), :], fmap_l[n, cols(t), :])
        state = select(t, state, jnp.zeros_like(state))
        f_split[t, :, lanes(n)] = stacked(state)

    if split:
        for t in down:
            for j in range(half):
                forward_state(t, base + j)
        for j in range(half):
            hand_copy(f_scan, j, other_base).wait_recv()

    merging = n_sp == 4 and nsub % 2 == 0
    mid = nsub // 2

    def product(q, t):
        full = folded(dot(f_split[t], diag[t, :, q * width : (q + 1) * width], ((1,), (0,))))
        for n in range(nsub):
            w_send[q, t, n] = full[:, cols(n)]

    def piece(h):
        return pl.ds(0, nsub) if h is None else pl.ds(h * mid, mid)

    def final(q, t, slot, h):
        sem = h or 0
        return remote(
            w_send.at[q, t, piece(h)], w_recv.at[slot, t, piece(h)],
            ws_sem.at[q, t, sem], wr_sem.at[slot, t, sem], {"space": q},
        )

    def passing(q, t, to, h):
        return remote(
            w_send.at[q, t, piece(h)], w_pass.at[t, piece(h)],
            ps_sem.at[t, h or 0], pr_sem.at[t], {"space": to},
        )

    def merge(q, t, h):
        passing(q, t, 0, h).wait_recv()
        for n in range(nsub) if h is None else range(h * mid, h * mid + mid):
            w_send[q, t, n] += w_pass[t, n]

    for t in down:
        for j in range(half):
            forward_state(t, other_base + j)

        if merging:

            @pl.when(p == 3)
            def _():
                product(0, t)
                passing(0, t, 2, 0).start()
                passing(0, t, 1, 1).start()

            @pl.when(p == 2)
            def _():
                product(1, t)
                passing(1, t, 3, None).start()
                product(0, t)
                final(0, t, 1, 1).start()

            @pl.when(p == 1)
            def _():
                product(0, t)
                final(0, t, 0, 0).start()

        else:
            for q in range(n_sp - 1):

                @pl.when(p > q)
                def _():
                    product(q, t)
                    final(q, t, p - 1, None).start()

    if merging:

        @pl.when(p == 3)
        def _():
            for t in down:
                product(2, t)
                final(2, t, 0, None).start()
                product(1, t)
                merge(1, t, None)
                final(1, t, 0, None).start()

        @pl.when(p == 2)
        def _():
            for t in down:
                merge(0, t, 0)
                final(0, t, 1, 0).start()

        @pl.when(p == 1)
        def _():
            for t in down:
                merge(0, t, 1)
                final(0, t, 0, 1).start()

    total = jnp.zeros((F, 2 * rows), F32)
    for t in range(T):
        total = total + dot(arrow[t], f_split[t], ((1,), (1,)))
    part[...] = total
    gath_sp[p] = total
    for d in range(1, n_sp):
        remote(part, gath_sp.at[p], as_sem.at[d - 1], ar_sem.at[p], {"space": lax.rem(p + d, n_sp)}).start()

    pl.when(chip < chips // 2)(early)
    map_copy(b_scan).wait_recv()
    join_maps(b_scan, 1, b_lead, -1)

    own_cols = pl.ds(pl.multiple_of(p * width, width), width)
    for t in range(T):
        block = diag[t, :, own_cols]
        full = folded(dot(f_split[t], block, ((1,), (0,))))
        arrow_full = dot(arrow[t], block, ((1,), (0,)))
        for n in range(nsub):
            g_loc[t, n] = full[:, cols(n)]
            v_own[t, n] = arrow_full[:, cols(n)]

    for d in range(1, n_sp):
        come = lax.rem(p + d, n_sp)
        remote(part, gath_sp.at[come], as_sem.at[d - 1], ar_sem.at[come], {"space": come}).wait_recv()
    total = gath_sp[0]
    for i in range(1, n_sp):
        total = total + gath_sp[i]
    mine_tm[...] = total
    gath_tm[s] = total
    for d in range(1, n_tm):
        remote(mine_tm, gath_tm.at[s], ts_sem.at[d - 1], tr_sem.at[s], {"tm": lax.rem(s + d, n_tm)}).start()

    for q in range(1, n_sp):

        @pl.when(p < q)
        def _():
            remote(v_send.at[0], v_recv.at[q - 1], vs_sem.at[0], vr_sem.at[q - 1], {"space": q}).wait_recv()
            for t in range(T):
                for n in range(nsub):
                    v_own[t, n] += v_recv[q - 1, t, n]

    for d in range(1, n_tm):
        come = lax.rem(s + d, n_tm)
        remote(mine_tm, gath_tm.at[come], ts_sem.at[d - 1], tr_sem.at[come], {"tm": come}).wait_recv()
    total = gath_tm[0]
    for i in range(1, n_tm):
        total = total + gath_tm[i]
    exact = functools.partial(
        lax.dot_general, preferred_element_type=F32, precision=lax.Precision.HIGHEST
    )
    side = tip_side[...] - total[:, :rows]
    tip_state = exact(tip_inv[...], side, (((1,), (0,)), ((), ())))
    turned = exact(tip_inv[...].T, tip_state, (((1,), (0,)), ((), ())))
    tip_out[...] = turned
    tip = turned.T

    for t in range(T):
        for n in range(nsub):
            g_loc[t, n] -= exact(tip, v_own[t, n], (((1,), (0,)), ((), ())))

    def take(t, slot, parts):
        for h in parts:
            final(0, t, slot, h).wait_recv()
        for n in range(nsub):
            g_loc[t, n] += w_recv[slot, t, n]

    for t in down:
        if merging:

            @pl.when(p == 0)
            def _():
                take(t, 0, (0, 1))
                take(t, 1, (0, 1))

            @pl.when(jnp.logical_or(p == 1, p == 2))
            def _():
                take(t, 0, (None,))

        else:
            for q in range(1, n_sp):
                pl.when(p < q)(functools.partial(take, t, q - 1, (None,)))

        for n in range(nsub):
            new = g_loc[t, n]
            if t < T - 1:
                old = g_loc[t + 1, n]
                new = select(t, new - couple(old, bc[t, cols(n), :]), old)
            else:
                new = select(t, new, jnp.zeros_like(new))
            g_loc[t, n] = new

    off_copy(b_scan, g_loc.at[0]).start()
    join_offsets(b_scan, g_loc.at[0], 1, b_lead, -1)
    chain(b_scan, b_first, b_last, 1, b_lead, -1)

    def backward_states(n):
        states = apply_map(b_scan["into"][n], bmap_h[n], bmap_l[n])
        for t in range(T):
            sol[t, :, lanes(n)] = g_loc[t, n] + states[:, cols(t)]

    if split:
        for j in range(half):
            backward_states(base + j)
        for j in range(half):
            hand_copy(b_scan, j, other_base).wait_recv()
    for j in range(half):
        backward_states(other_base + j)

    scan_end(f_scan, driven.at[T - 1], f_last, f_lead, 1)
    scan_end(b_scan, g_loc.at[0], b_last, b_lead, -1)
    for q in range(n_sp - 1):

        @pl.when(p > q)
        def _():
            remote(v_send.at[q], v_recv.at[p - 1], vs_sem.at[q], vr_sem.at[p - 1], {"space": q}).wait_send()
            if not merging:
                for t in down:
                    final(q, t, p - 1, None).wait_send()

    if merging:

        @pl.when(p == 3)
        def _():
            for t in down:
                passing(0, t, 2, 0).wait_send()
                passing(0, t, 1, 1).wait_send()
                final(2, t, 0, None).wait_send()
                final(1, t, 0, None).wait_send()

        @pl.when(p == 2)
        def _():
            for t in down:
                passing(1, t, 3, None).wait_send()
                final(0, t, 1, 0).wait_send()
                final(0, t, 1, 1).wait_send()

        @pl.when(p == 1)
        def _():
            for t in down:
                final(0, t, 0, 0).wait_send()
                final(0, t, 0, 1).wait_send()

    for d in range(1, n_sp):
        remote(part, gath_sp.at[p], as_sem.at[d - 1], ar_sem.at[p], {"space": lax.rem(p + d, n_sp)}).wait_send()
    for d in range(1, n_tm):
        remote(mine_tm, gath_tm.at[s], ts_sem.at[d - 1], tr_sem.at[s], {"tm": lax.rem(s + d, n_tm)}).wait_send()


def finish(sec, states, turned, sol, tip):
    length = sec[lax.axis_index("tm")]
    for t in range(states.shape[0]):
        live = jnp.full(states.shape[1:], length, jnp.int32) > t
        sol[t] = jnp.where(live, states[t], jnp.zeros_like(states[t]))
    tip[...] = turned[...]


def scan_scratch(nsub, rows, sub):
    half = nsub // 2 if nsub % 2 == 0 else nsub
    return {
        "map": pltpu.VMEM((nsub, sub, sub), F32),
        "mate_map": pltpu.VMEM((half, sub, sub), F32),
        "chip_map": pltpu.VMEM((half, sub, sub), F32),
        "chip_h": pltpu.VMEM((half, sub, sub), BF16),
        "chip_l": pltpu.VMEM((half, sub, sub), BF16),
        "one_h": pltpu.VMEM((half, sub, sub), BF16),
        "one_l": pltpu.VMEM((half, sub, sub), BF16),
        "ahead_map": pltpu.VMEM((half, sub, sub), F32),
        "mate_off": pltpu.VMEM((half, rows, sub), F32),
        "chip_off": pltpu.VMEM((half, rows, sub), F32),
        "one_off": pltpu.VMEM((half, rows, sub), F32),
        "ahead_off": pltpu.VMEM((half, rows, sub), F32),
        "chip_in": pltpu.VMEM((half, rows, sub), F32),
        "arrived": pltpu.VMEM((half, rows, sub), F32),
        "out": pltpu.VMEM((half, rows, sub), F32),
        "hand": pltpu.VMEM((half, rows, sub), F32),
        "into": pltpu.VMEM((nsub, rows, sub), F32),
        "sem": pltpu.SemaphoreType.DMA((2, 3 + 4 * half)),
    }


def on_device(n_tm, n_sp, sections, right_side, tip_side, diag_inverse, fwd, bwd, arrow_rows, tip_inverse):
    T, rows, total_width = right_side.shape
    width, sub = fwd.shape[1], fwd.shape[2]
    nsub = width // sub
    F = arrow_rows.shape[1]
    vmem, hbm = pl.BlockSpec(memory_space=pltpu.VMEM), pl.BlockSpec(memory_space=pl.ANY)
    maps = pltpu.VMEM((nsub, T * sub, sub), BF16)
    dma = pltpu.SemaphoreType.DMA
    others = n_sp - 1
    states, turned = pl.pallas_call(
        functools.partial(kernel, n_tm, n_sp),
        out_shape=(
            jax.ShapeDtypeStruct((T, rows, width), F32),
            jax.ShapeDtypeStruct(tip_side.shape[::-1], F32),
        ),
        in_specs=[
            pl.BlockSpec(memory_space=pltpu.SMEM),
            hbm,
            vmem,
            hbm,
            hbm,
            hbm,
            vmem,
            vmem,
        ],
        out_specs=(vmem, vmem),
        scratch_shapes=[
            pltpu.VMEM(right_side.shape, BF16),
            pltpu.VMEM(fwd.shape, BF16),
            pltpu.VMEM(bwd.shape, BF16),
            pltpu.VMEM(diag_inverse.shape, BF16),
            maps,
            maps,
            maps,
            maps,
            pltpu.VMEM((T, nsub, rows, sub), F32),
            pltpu.VMEM((T, 2 * rows, width), BF16),
            pltpu.VMEM((T, nsub, rows, sub), F32),
            pltpu.VMEM((others, T, nsub, rows, sub), F32),
            pltpu.VMEM((others, T, nsub, rows, sub), F32),
            pltpu.VMEM((T, nsub, rows, sub), F32),
            pltpu.VMEM((others, T, nsub, F, sub), F32),
            pltpu.VMEM((others, T, nsub, F, sub), F32),
            pltpu.VMEM((T, nsub, F, sub), F32),
            pltpu.VMEM((F, 2 * rows), F32),
            pltpu.VMEM((n_sp, F, 2 * rows), F32),
            pltpu.VMEM((n_tm, F, 2 * rows), F32),
            pltpu.VMEM((F, 2 * rows), F32),
            scan_scratch(nsub, rows, sub),
            scan_scratch(nsub, rows, sub),
            dma((3,)),
            dma((T,)),
            dma((others, T, 2)),
            dma((others, T, 2)),
            dma((T, 2)),
            dma((T,)),
            dma((others,)),
            dma((others,)),
            dma((others,)),
            dma((n_sp,)),
            dma((n_tm - 1,)),
            dma((n_tm,)),
        ],
        compiler_params=pltpu.CompilerParams(
            collective_id=0, has_side_effects=True, vmem_limit_bytes=56 * 1024 * 1024
        ),
        cost_estimate=pl.CostEstimate(
            flops=8 * T * rows * width * total_width, bytes_accessed=2 * diag_inverse.size, transcendentals=0
        ),
    )(sections, right_side, tip_side.T, diag_inverse, fwd, bwd, arrow_rows, tip_inverse)
    states, turned = pl.pallas_call(
        finish,
        out_shape=(
            jax.ShapeDtypeStruct(states.shape, F32),
            jax.ShapeDtypeStruct(turned.shape, F32),
        ),
        in_specs=[pl.BlockSpec(memory_space=pltpu.SMEM), vmem, vmem],
        out_specs=(vmem, vmem),
    )(sections, states, turned)
    return states, turned.T


def solution(mesh):
    placed = (
        P(),
        P("tm", None, None),
        P(),
        P("tm", "space", None),
        P("tm", "space", None),
        P("tm", "space", None),
        P("tm", None, "space"),
        P(),
    )
    return jax.shard_map(
        functools.partial(on_device, mesh.shape["tm"], mesh.shape["space"]),
        mesh=mesh,
        in_specs=placed,
        out_specs=(P("tm", None, "space"), P()),
        check_vma=False,
    )
```

```python
import functools

import jax
import jax.numpy as jnp
from jax import lax
from jax.experimental import pallas as pl
from jax.experimental.pallas import tpu as pltpu
from jax.sharding import PartitionSpec as P

F32 = jnp.float32
BF16 = jnp.bfloat16
MESH = pl.DeviceIdType.MESH


def dot(a, b, contract):
    return lax.dot_general(a, b, (contract, ((), ())), preferred_element_type=F32)


def stacked(x):
    high = x.astype(BF16).astype(F32)
    return jnp.concatenate([high, x - high], 0).astype(BF16)


def folded(y):
    rows = y.shape[0] // 2
    return y[:rows] + y[rows:]


def couple(x, block):
    return folded(dot(stacked(x), block, ((1,), (1,))))


def halves(x):
    high = x.astype(BF16)
    return high, (x - high.astype(F32)).astype(BF16)


def apply_map(x, high, low):
    rows = x.shape[0]
    pieces = stacked(x)
    return folded(dot(pieces, high, ((1,), (0,)))) + dot(pieces[:rows], low, ((1,), (0,)))


def kernel(
    n_tm, n_sp, sec, rs_hbm, tip_side, diag_hbm, fc_hbm, bc_hbm, arrow, tip_inv,
    sol, tip_out,
    rs, fc, bc, diag, fmap_h, fmap_l, bmap_h, bmap_l, driven, f_split, g_loc,
    w_send, w_recv, w_pass, v_send, v_recv, v_own, part, gath_sp, gath_tm, mine_tm,
    f_scan, b_scan,
    in_sem, diag_sem, ws_sem, wr_sem, ps_sem, pr_sem, vs_sem, vr_sem, as_sem, ar_sem, ts_sem, tr_sem,
):
    T, rows = rs_hbm.shape[0], rs_hbm.shape[1]
    width, sub = fc_hbm.shape[1], fc_hbm.shape[2]
    nsub = width // sub
    F = arrow.shape[1]
    s, p = lax.axis_index("tm"), lax.axis_index("space")
    core, chip, chips = lax.rem(s, 2), s // 2, n_tm // 2
    length = sec[s]
    half, split = (nsub // 2, True) if nsub % 2 == 0 else (nsub, False)
    base = core * half if split else 0
    other_base = half - core * half if split else 0
    mate = s + 1 - 2 * core

    first_loads = [
        pltpu.make_async_copy(src, dst, in_sem.at[i])
        for i, (src, dst) in enumerate(((fc_hbm, fc), (bc_hbm, bc), (rs_hbm, rs)))
    ]
    loads = [
        pltpu.make_async_copy(diag_hbm.at[t], diag.at[t], diag_sem.at[t]) for t in range(T)
    ]
    for load in first_loads + loads:
        load.start()

    barrier = pltpu.get_barrier_semaphore()
    for d in range(1, n_tm):
        pl.semaphore_signal(barrier, inc=1, device_id={"tm": lax.rem(s + d, n_tm)}, device_id_type=MESH)
    for d in range(1, n_sp):
        pl.semaphore_signal(barrier, inc=1, device_id={"space": lax.rem(p + d, n_sp)}, device_id_type=MESH)

    def cols(n):
        return slice(n * sub, (n + 1) * sub)

    def select(t, new, old):
        if t == 0:
            return new
        return jnp.where(jnp.full(new.shape, length, jnp.int32) > t, new, old)

    def remote(src, dst, send, recv, to):
        return pltpu.make_async_remote_copy(
            src_ref=src, dst_ref=dst, send_sem=send, recv_sem=recv, device_id=to, device_id_type=MESH
        )

    def section_maps(jobs):
        row = lax.broadcasted_iota(jnp.int32, (sub, sub), 0)
        col = lax.broadcasted_iota(jnp.int32, (sub, sub), 1)
        eye = jnp.where(row == col, 1.0, 0.0)
        maps = [[eye.astype(F32)] * nsub for _ in jobs]
        for i in range(T):
            for own, (coupling, order, high_ref, low_ref, _) in zip(maps, jobs):
                t = order[i]
                for n in range(nsub):
                    block = coupling[t, cols(n), :]
                    if i == 0:
                        new = -dot(eye.astype(BF16), block, ((1,), (1,)))
                    else:
                        new = -couple(own[n], block)
                    own[n] = select(t, new, own[n])
                    high_ref[n, :, cols(t)], low_ref[n, :, cols(t)] = halves(own[n])
        for own, job in zip(maps, jobs):
            for n in range(nsub):
                job[4][n] = own[n]

    def in_order(mine, theirs, lead):
        ahead = jnp.full(mine.shape, core, jnp.int32) == lead
        return jnp.where(ahead, mine, theirs), jnp.where(ahead, theirs, mine)

    def map_copy(scan):
        return remote(
            scan["map"].at[pl.ds(other_base, half)], scan["mate_map"],
            scan["sem"].at[0, 0], scan["sem"].at[1, 0], {"tm": mate},
        )

    def off_copy(scan, own):
        return remote(
            own.at[pl.ds(other_base, half)], scan["mate_off"],
            scan["sem"].at[0, 1], scan["sem"].at[1, 1], {"tm": mate},
        )

    def pair_map_copy(scan, way):
        return remote(
            scan["chip_map"], scan["ahead_map"],
            scan["sem"].at[0, 2 + 2 * half], scan["sem"].at[1, 2 + 2 * half], {"tm": away(way, 2)},
        )

    def pair_off_copy(scan, j, way):
        at = 3 + 2 * half + j
        return remote(
            scan["chip_off"].at[j], scan["ahead_off"].at[j],
            scan["sem"].at[0, at], scan["sem"].at[1, at], {"tm": away(way, 2)},
        )

    def away(way, steps):
        return lax.rem(s + n_tm + way * steps, n_tm)

    def join_maps(scan, lead, first_of_pair, way):
        for j in range(half):
            one, two = in_order(scan["map"][base + j], scan["mate_map"][j], lead)
            scan["one_h"][j], scan["one_l"][j] = halves(one)
            both = apply_map(one, *halves(two))
            scan["chip_map"][j] = both
            scan["chip_h"][j], scan["chip_l"][j] = halves(both)
        pl.when(first_of_pair)(pair_map_copy(scan, way).start)

    def join_offsets(scan, own, lead, first_of_pair, way):
        off_copy(scan, own).wait_recv()
        for j in range(half):
            _, after = in_order(scan["map"][base + j], scan["mate_map"][j], lead)
            one, two = in_order(own[base + j], scan["mate_off"][j], lead)
            scan["chip_off"][j] = two + apply_map(one, *halves(after))
            scan["one_off"][j] = one
            pl.when(first_of_pair)(pair_off_copy(scan, j, way).start)

    def hop_copy(scan, j, to, far):
        at = 3 + 3 * half + j if far else 2 + j
        return remote(
            scan["out"].at[j], scan["arrived"].at[j],
            scan["sem"].at[0, at], scan["sem"].at[1, 2 + j], {"tm": to},
        )

    def hand_copy(scan, j, at):
        return remote(
            scan["hand"].at[j], scan["into"].at[at + j],
            scan["sem"].at[0, 2 + half + j], scan["sem"].at[1, 2 + half + j], {"tm": mate},
        )

    def chain(scan, first, last, lead, first_of_pair, way):
        second = jnp.logical_not(first_of_pair)
        later = jnp.logical_not(first)

        @pl.when(jnp.logical_and(second, later))
        def _():
            pair_map_copy(scan, way).wait_recv()

        for j in range(half):

            @pl.when(second)
            def _():
                pair_off_copy(scan, j, way).wait_recv()
                scan["chip_in"][j] = scan["ahead_off"][j]

            @pl.when(jnp.logical_and(first_of_pair, first))
            def _():
                scan["chip_in"][j] = jnp.zeros((rows, sub), F32)

            pl.when(later)(hop_copy(scan, j, mate, False).wait_recv)

            @pl.when(jnp.logical_and(first_of_pair, later))
            def _():
                scan["chip_in"][j] = scan["arrived"][j]

            @pl.when(jnp.logical_and(second, later))
            def _():
                scan["chip_in"][j] += apply_map(scan["arrived"][j], *halves(scan["ahead_map"][j]))

            @pl.when(jnp.logical_and(second, jnp.logical_not(last)))
            def _():
                after = apply_map(scan["chip_in"][j], scan["chip_h"][j], scan["chip_l"][j])
                scan["out"][j] = scan["chip_off"][j] + after
                hop_copy(scan, j, away(way, 4), True).start()
                hop_copy(scan, j, away(way, 2), False).start()

        for j in range(half):
            chip_in = scan["chip_in"][j]
            after = apply_map(chip_in, scan["one_h"][j], scan["one_l"][j])
            mine, theirs = in_order(chip_in, scan["one_off"][j] + after, lead)
            if split:
                scan["hand"][j] = theirs
                hand_copy(scan, j, base).start()
            scan["into"][base + j] = mine

        @pl.when(jnp.logical_and(second, first))
        def _():
            pair_map_copy(scan, way).wait_recv()

    def scan_end(scan, own, last, first_of_pair, way):
        map_copy(scan).wait_send()
        off_copy(scan, own).wait_send()

        @pl.when(first_of_pair)
        def _():
            pair_map_copy(scan, way).wait_send()
            for j in range(half):
                pair_off_copy(scan, j, way).wait_send()

        @pl.when(jnp.logical_not(jnp.logical_or(first_of_pair, last)))
        def _():
            for j in range(half):
                hop_copy(scan, j, away(way, 4), True).wait_send()
                hop_copy(scan, j, away(way, 2), False).wait_send()

        if split:
            for j in range(half):
                hand_copy(scan, j, base).wait_send()

    f_first, f_last = chip // 2 == 0, chip // 2 == chips // 2 - 1
    b_first, b_last = f_last, f_first
    f_lead, b_lead = lax.rem(chip, 2) == 0, lax.rem(chip, 2) == 1

    up, down = list(range(T)), list(range(T - 1, -1, -1))
    first_loads[0].wait()
    first_loads[1].wait()
    section_maps(((fc, up, fmap_h, fmap_l, f_scan["map"]), (bc, down, bmap_h, bmap_l, b_scan["map"])))
    first_loads[2].wait()
    carry = [None] * nsub
    for t in range(T):
        loads[t].wait()
        full = dot(rs[t], diag[t], ((1,), (1,)))
        for n in range(nsub):
            new = full[:, cols(n)]
            if t > 0:
                new = select(t, new - couple(carry[n], fc[t, cols(n), :]), carry[n])
            carry[n] = new
            driven[t, n] = new
    pl.semaphore_wait(barrier, n_tm - 1 + n_sp - 1)
    map_copy(f_scan).start()
    off_copy(f_scan, driven.at[T - 1]).start()
    map_copy(b_scan).start()
    map_copy(f_scan).wait_recv()
    join_offsets(f_scan, driven.at[T - 1], 0, f_lead, 1)
    join_maps(f_scan, 0, f_lead, 1)

    def early():
        for q in range(n_sp - 1):

            @pl.when(p > q)
            def _():
                for t in range(T):
                    full = dot(arrow[t], diag[t, :, q * width : (q + 1) * width], ((1,), (0,)))
                    for n in range(nsub):
                        v_send[q, t, n] = full[:, cols(n)]
                remote(v_send.at[q], v_recv.at[p - 1], vs_sem.at[q], vr_sem.at[p - 1], {"space": q}).start()

    pl.when(chip >= chips // 2)(early)

    chain(f_scan, f_first, f_last, 0, f_lead, 1)

    if split:
        for j in range(half):
            hand_copy(f_scan, j, other_base).wait_recv()

    merging = n_sp == 4 and nsub % 2 == 0
    mid = nsub // 2

    def product(q, t):
        full = folded(dot(f_split[t], diag[t, :, q * width : (q + 1) * width], ((1,), (0,))))
        for n in range(nsub):
            w_send[q, t, n] = full[:, cols(n)]

    def piece(h):
        return pl.ds(0, nsub) if h is None else pl.ds(h * mid, mid)

    def final(q, t, slot, h):
        sem = h or 0
        return remote(
            w_send.at[q, t, piece(h)], w_recv.at[slot, t, piece(h)],
            ws_sem.at[q, t, sem], wr_sem.at[slot, t, sem], {"space": q},
        )

    def passing(q, t, to, h):
        return remote(
            w_send.at[q, t, piece(h)], w_pass.at[t, piece(h)],
            ps_sem.at[t, h or 0], pr_sem.at[t], {"space": to},
        )

    def merge(q, t, h):
        passing(q, t, 0, h).wait_recv()
        for n in range(nsub) if h is None else range(h * mid, h * mid + mid):
            w_send[q, t, n] += w_pass[t, n]

    for t in down:
        for n in range(nsub):
            state = driven[t, n] + apply_map(f_scan["into"][n], fmap_h[n, :, cols(t)], fmap_l[n, :, cols(t)])
            state = select(t, state, jnp.zeros_like(state))
            f_split[t, :, cols(n)] = stacked(state)

        if merging:

            @pl.when(p == 3)
            def _():
                product(0, t)
                passing(0, t, 2, 0).start()
                passing(0, t, 1, 1).start()

            @pl.when(p == 2)
            def _():
                product(1, t)
                passing(1, t, 3, None).start()
                product(0, t)
                final(0, t, 1, 1).start()

            @pl.when(p == 1)
            def _():
                product(0, t)
                final(0, t, 0, 0).start()

        else:
            for q in range(n_sp - 1):

                @pl.when(p > q)
                def _():
                    product(q, t)
                    final(q, t, p - 1, None).start()

    if merging:

        @pl.when(p == 3)
        def _():
            for t in down:
                product(2, t)
                final(2, t, 0, None).start()
                product(1, t)
                merge(1, t, None)
                final(1, t, 0, None).start()

        @pl.when(p == 2)
        def _():
            for t in down:
                merge(0, t, 0)
                final(0, t, 1, 0).start()

        @pl.when(p == 1)
        def _():
            for t in down:
                merge(0, t, 1)
                final(0, t, 0, 1).start()

    total = jnp.zeros((F, 2 * rows), F32)
    for t in range(T):
        total = total + dot(arrow[t], f_split[t], ((1,), (1,)))
    part[...] = total
    gath_sp[p] = total
    for d in range(1, n_sp):
        remote(part, gath_sp.at[p], as_sem.at[d - 1], ar_sem.at[p], {"space": lax.rem(p + d, n_sp)}).start()

    pl.when(chip < chips // 2)(early)
    map_copy(b_scan).wait_recv()
    join_maps(b_scan, 1, b_lead, -1)

    own_cols = pl.ds(pl.multiple_of(p * width, width), width)
    for t in range(T):
        block = diag[t, :, own_cols]
        full = folded(dot(f_split[t], block, ((1,), (0,))))
        arrow_full = dot(arrow[t], block, ((1,), (0,)))
        for n in range(nsub):
            g_loc[t, n] = full[:, cols(n)]
            v_own[t, n] = arrow_full[:, cols(n)]

    for d in range(1, n_sp):
        come = lax.rem(p + d, n_sp)
        remote(part, gath_sp.at[come], as_sem.at[d - 1], ar_sem.at[come], {"space": come}).wait_recv()
    total = gath_sp[0]
    for i in range(1, n_sp):
        total = total + gath_sp[i]
    mine_tm[...] = total
    gath_tm[s] = total
    for d in range(1, n_tm):
        remote(mine_tm, gath_tm.at[s], ts_sem.at[d - 1], tr_sem.at[s], {"tm": lax.rem(s + d, n_tm)}).start()

    for q in range(1, n_sp):

        @pl.when(p < q)
        def _():
            remote(v_send.at[0], v_recv.at[q - 1], vs_sem.at[0], vr_sem.at[q - 1], {"space": q}).wait_recv()
            for t in range(T):
                for n in range(nsub):
                    v_own[t, n] += v_recv[q - 1, t, n]

    for d in range(1, n_tm):
        come = lax.rem(s + d, n_tm)
        remote(mine_tm, gath_tm.at[come], ts_sem.at[d - 1], tr_sem.at[come], {"tm": come}).wait_recv()
    total = gath_tm[0]
    for i in range(1, n_tm):
        total = total + gath_tm[i]
    exact = functools.partial(
        lax.dot_general, preferred_element_type=F32, precision=lax.Precision.HIGHEST
    )
    side = tip_side[...] - total[:, :rows]
    tip_state = exact(tip_inv[...], side, (((1,), (0,)), ((), ())))
    turned = exact(tip_inv[...].T, tip_state, (((1,), (0,)), ((), ())))
    tip_out[...] = turned
    tip = turned.T

    for t in range(T):
        for n in range(nsub):
            g_loc[t, n] -= exact(tip, v_own[t, n], (((1,), (0,)), ((), ())))

    def take(t, slot, parts):
        for h in parts:
            final(0, t, slot, h).wait_recv()
        for n in range(nsub):
            g_loc[t, n] += w_recv[slot, t, n]

    for t in down:
        if merging:

            @pl.when(p == 0)
            def _():
                take(t, 0, (0, 1))
                take(t, 1, (0, 1))

            @pl.when(jnp.logical_or(p == 1, p == 2))
            def _():
                take(t, 0, (None,))

        else:
            for q in range(1, n_sp):
                pl.when(p < q)(functools.partial(take, t, q - 1, (None,)))

        for n in range(nsub):
            new = g_loc[t, n]
            if t < T - 1:
                old = g_loc[t + 1, n]
                new = select(t, new - couple(old, bc[t, cols(n), :]), old)
            else:
                new = select(t, new, jnp.zeros_like(new))
            g_loc[t, n] = new

    off_copy(b_scan, g_loc.at[0]).start()
    join_offsets(b_scan, g_loc.at[0], 1, b_lead, -1)
    chain(b_scan, b_first, b_last, 1, b_lead, -1)

    if split:
        for j in range(half):
            hand_copy(b_scan, j, other_base).wait_recv()
    for n in range(nsub):
        states = apply_map(b_scan["into"][n], bmap_h[n], bmap_l[n])
        for t in range(T):
            sol[t, :, cols(n)] = g_loc[t, n] + states[:, cols(t)]

    scan_end(f_scan, driven.at[T - 1], f_last, f_lead, 1)
    scan_end(b_scan, g_loc.at[0], b_last, b_lead, -1)
    for q in range(n_sp - 1):

        @pl.when(p > q)
        def _():
            remote(v_send.at[q], v_recv.at[p - 1], vs_sem.at[q], vr_sem.at[p - 1], {"space": q}).wait_send()
            if not merging:
                for t in down:
                    final(q, t, p - 1, None).wait_send()

    if merging:

        @pl.when(p == 3)
        def _():
            for t in down:
                passing(0, t, 2, 0).wait_send()
                passing(0, t, 1, 1).wait_send()
                final(2, t, 0, None).wait_send()
                final(1, t, 0, None).wait_send()

        @pl.when(p == 2)
        def _():
            for t in down:
                passing(1, t, 3, None).wait_send()
                final(0, t, 1, 0).wait_send()
                final(0, t, 1, 1).wait_send()

        @pl.when(p == 1)
        def _():
            for t in down:
                final(0, t, 0, 0).wait_send()
                final(0, t, 0, 1).wait_send()

    for d in range(1, n_sp):
        remote(part, gath_sp.at[p], as_sem.at[d - 1], ar_sem.at[p], {"space": lax.rem(p + d, n_sp)}).wait_send()
    for d in range(1, n_tm):
        remote(mine_tm, gath_tm.at[s], ts_sem.at[d - 1], tr_sem.at[s], {"tm": lax.rem(s + d, n_tm)}).wait_send()


def finish(sec, states, turned, sol, tip):
    length = sec[lax.axis_index("tm")]
    for t in range(states.shape[0]):
        live = jnp.full(states.shape[1:], length, jnp.int32) > t
        sol[t] = jnp.where(live, states[t], jnp.zeros_like(states[t]))
    tip[...] = turned[...]


def scan_scratch(nsub, rows, sub):
    half = nsub // 2 if nsub % 2 == 0 else nsub
    return {
        "map": pltpu.VMEM((nsub, sub, sub), F32),
        "mate_map": pltpu.VMEM((half, sub, sub), F32),
        "chip_map": pltpu.VMEM((half, sub, sub), F32),
        "chip_h": pltpu.VMEM((half, sub, sub), BF16),
        "chip_l": pltpu.VMEM((half, sub, sub), BF16),
        "one_h": pltpu.VMEM((half, sub, sub), BF16),
        "one_l": pltpu.VMEM((half, sub, sub), BF16),
        "ahead_map": pltpu.VMEM((half, sub, sub), F32),
        "mate_off": pltpu.VMEM((half, rows, sub), F32),
        "chip_off": pltpu.VMEM((half, rows, sub), F32),
        "one_off": pltpu.VMEM((half, rows, sub), F32),
        "ahead_off": pltpu.VMEM((half, rows, sub), F32),
        "chip_in": pltpu.VMEM((half, rows, sub), F32),
        "arrived": pltpu.VMEM((half, rows, sub), F32),
        "out": pltpu.VMEM((half, rows, sub), F32),
        "hand": pltpu.VMEM((half, rows, sub), F32),
        "into": pltpu.VMEM((nsub, rows, sub), F32),
        "sem": pltpu.SemaphoreType.DMA((2, 3 + 4 * half)),
    }


def on_device(n_tm, n_sp, sections, right_side, tip_side, diag_inverse, fwd, bwd, arrow_rows, tip_inverse):
    T, rows, total_width = right_side.shape
    width, sub = fwd.shape[1], fwd.shape[2]
    nsub = width // sub
    F = arrow_rows.shape[1]
    vmem, hbm = pl.BlockSpec(memory_space=pltpu.VMEM), pl.BlockSpec(memory_space=pl.ANY)
    maps = pltpu.VMEM((nsub, sub, T * sub), BF16)
    dma = pltpu.SemaphoreType.DMA
    others = n_sp - 1
    states, turned = pl.pallas_call(
        functools.partial(kernel, n_tm, n_sp),
        out_shape=(
            jax.ShapeDtypeStruct((T, rows, width), F32),
            jax.ShapeDtypeStruct(tip_side.shape[::-1], F32),
        ),
        in_specs=[
            pl.BlockSpec(memory_space=pltpu.SMEM),
            hbm,
            vmem,
            hbm,
            hbm,
            hbm,
            vmem,
            vmem,
        ],
        out_specs=(vmem, vmem),
        scratch_shapes=[
            pltpu.VMEM(right_side.shape, BF16),
            pltpu.VMEM(fwd.shape, BF16),
            pltpu.VMEM(bwd.shape, BF16),
            pltpu.VMEM(diag_inverse.shape, BF16),
            maps,
            maps,
            maps,
            maps,
            pltpu.VMEM((T, nsub, rows, sub), F32),
            pltpu.VMEM((T, 2 * rows, width), BF16),
            pltpu.VMEM((T, nsub, rows, sub), F32),
            pltpu.VMEM((others, T, nsub, rows, sub), F32),
            pltpu.VMEM((others, T, nsub, rows, sub), F32),
            pltpu.VMEM((T, nsub, rows, sub), F32),
            pltpu.VMEM((others, T, nsub, F, sub), F32),
            pltpu.VMEM((others, T, nsub, F, sub), F32),
            pltpu.VMEM((T, nsub, F, sub), F32),
            pltpu.VMEM((F, 2 * rows), F32),
            pltpu.VMEM((n_sp, F, 2 * rows), F32),
            pltpu.VMEM((n_tm, F, 2 * rows), F32),
            pltpu.VMEM((F, 2 * rows), F32),
            scan_scratch(nsub, rows, sub),
            scan_scratch(nsub, rows, sub),
            dma((3,)),
            dma((T,)),
            dma((others, T, 2)),
            dma((others, T, 2)),
            dma((T, 2)),
            dma((T,)),
            dma((others,)),
            dma((others,)),
            dma((others,)),
            dma((n_sp,)),
            dma((n_tm - 1,)),
            dma((n_tm,)),
        ],
        compiler_params=pltpu.CompilerParams(
            collective_id=0, has_side_effects=True, vmem_limit_bytes=56 * 1024 * 1024
        ),
        cost_estimate=pl.CostEstimate(
            flops=8 * T * rows * width * total_width, bytes_accessed=2 * diag_inverse.size, transcendentals=0
        ),
    )(sections, right_side, tip_side.T, diag_inverse, fwd, bwd, arrow_rows, tip_inverse)
    states, turned = pl.pallas_call(
        finish,
        out_shape=(
            jax.ShapeDtypeStruct(states.shape, F32),
            jax.ShapeDtypeStruct(turned.shape, F32),
        ),
        in_specs=[pl.BlockSpec(memory_space=pltpu.SMEM), vmem, vmem],
        out_specs=(vmem, vmem),
    )(sections, states, turned)
    return states, turned.T


def solution(mesh):
    placed = (
        P(),
        P("tm", None, None),
        P(),
        P("tm", "space", None),
        P("tm", "space", None),
        P("tm", "space", None),
        P("tm", None, "space"),
        P(),
    )
    return jax.shard_map(
        functools.partial(on_device, mesh.shape["tm"], mesh.shape["space"]),
        mesh=mesh,
        in_specs=placed,
        out_specs=(P("tm", None, "space"), P()),
        check_vma=False,
    )
```

```python
import functools

import jax
import jax.numpy as jnp
from jax import lax
from jax.experimental import pallas as pl
from jax.experimental.pallas import tpu as pltpu
from jax.sharding import PartitionSpec as P

F32 = jnp.float32
BF16 = jnp.bfloat16
MESH = pl.DeviceIdType.MESH


def dot(a, b, contract):
    return lax.dot_general(a, b, (contract, ((), ())), preferred_element_type=F32)


def stacked(x):
    high = x.astype(BF16).astype(F32)
    return jnp.concatenate([high, x - high], 0).astype(BF16)


def folded(y):
    rows = y.shape[0] // 2
    return y[:rows] + y[rows:]


def couple(x, block):
    return folded(dot(stacked(x), block, ((1,), (1,))))


def halves(x):
    high = x.astype(BF16)
    return high, (x - high.astype(F32)).astype(BF16)


def apply_map(x, high, low):
    rows = x.shape[0]
    pieces = stacked(x)
    return folded(dot(pieces, high, ((1,), (0,)))) + dot(pieces[:rows], low, ((1,), (0,)))


def kernel(
    n_tm, n_sp, sec, rs, tip_side, diag_hbm, fc, bc, arrow, tip_inv,
    sol, tip_out,
    diag, fmap_h, fmap_l, bmap_h, bmap_l, driven, f_split, g_loc,
    w_send, w_recv, w_pass, v_send, v_recv, v_own, part, gath_sp, gath_tm, mine_tm,
    f_scan, b_scan,
    diag_sem, ws_sem, wr_sem, ps_sem, pr_sem, vs_sem, vr_sem, as_sem, ar_sem, ts_sem, tr_sem,
):
    T, rows = rs.shape[0], rs.shape[1]
    width, sub = fc.shape[1], fc.shape[2]
    nsub = width // sub
    F = arrow.shape[1]
    s, p = lax.axis_index("tm"), lax.axis_index("space")
    core, chip, chips = lax.rem(s, 2), s // 2, n_tm // 2
    length = sec[s]
    half, split = (nsub // 2, True) if nsub % 2 == 0 else (nsub, False)
    base = core * half if split else 0
    other_base = half - core * half if split else 0
    mate = s + 1 - 2 * core

    loads = [
        pltpu.make_async_copy(diag_hbm.at[t], diag.at[t], diag_sem.at[t]) for t in range(T)
    ]
    for load in loads:
        load.start()

    barrier = pltpu.get_barrier_semaphore()
    for d in range(1, n_tm):
        pl.semaphore_signal(barrier, inc=1, device_id={"tm": lax.rem(s + d, n_tm)}, device_id_type=MESH)
    for d in range(1, n_sp):
        pl.semaphore_signal(barrier, inc=1, device_id={"space": lax.rem(p + d, n_sp)}, device_id_type=MESH)

    def cols(n):
        return slice(n * sub, (n + 1) * sub)

    def select(t, new, old):
        if t == 0:
            return new
        return jnp.where(jnp.full(new.shape, length, jnp.int32) > t, new, old)

    def remote(src, dst, send, recv, to):
        return pltpu.make_async_remote_copy(
            src_ref=src, dst_ref=dst, send_sem=send, recv_sem=recv, device_id=to, device_id_type=MESH
        )

    def section_maps(jobs):
        row = lax.broadcasted_iota(jnp.int32, (sub, sub), 0)
        col = lax.broadcasted_iota(jnp.int32, (sub, sub), 1)
        eye = jnp.where(row == col, 1.0, 0.0)
        maps = [[eye.astype(F32)] * nsub for _ in jobs]
        for i in range(T):
            for own, (coupling, order, high_ref, low_ref, _) in zip(maps, jobs):
                t = order[i]
                for n in range(nsub):
                    block = coupling[t, cols(n), :]
                    if i == 0:
                        new = -dot(eye.astype(BF16), block, ((1,), (1,)))
                    else:
                        new = -couple(own[n], block)
                    own[n] = select(t, new, own[n])
                    high_ref[n, :, cols(t)], low_ref[n, :, cols(t)] = halves(own[n])
        for own, job in zip(maps, jobs):
            for n in range(nsub):
                job[4][n] = own[n]

    def in_order(mine, theirs, lead):
        ahead = jnp.full(mine.shape, core, jnp.int32) == lead
        return jnp.where(ahead, mine, theirs), jnp.where(ahead, theirs, mine)

    def map_copy(scan):
        return remote(
            scan["map"].at[pl.ds(other_base, half)], scan["mate_map"],
            scan["sem"].at[0, 0], scan["sem"].at[1, 0], {"tm": mate},
        )

    def off_copy(scan, own):
        return remote(
            own.at[pl.ds(other_base, half)], scan["mate_off"],
            scan["sem"].at[0, 1], scan["sem"].at[1, 1], {"tm": mate},
        )

    def pair_map_copy(scan, way):
        return remote(
            scan["chip_map"], scan["ahead_map"],
            scan["sem"].at[0, 2 + 2 * half], scan["sem"].at[1, 2 + 2 * half], {"tm": away(way, 2)},
        )

    def pair_off_copy(scan, j, way):
        at = 3 + 2 * half + j
        return remote(
            scan["chip_off"].at[j], scan["ahead_off"].at[j],
            scan["sem"].at[0, at], scan["sem"].at[1, at], {"tm": away(way, 2)},
        )

    def away(way, steps):
        return lax.rem(s + n_tm + way * steps, n_tm)

    def join_maps(scan, lead, first_of_pair, way):
        for j in range(half):
            one, two = in_order(scan["map"][base + j], scan["mate_map"][j], lead)
            scan["one_h"][j], scan["one_l"][j] = halves(one)
            both = apply_map(one, *halves(two))
            scan["chip_map"][j] = both
            scan["chip_h"][j], scan["chip_l"][j] = halves(both)
        pl.when(first_of_pair)(pair_map_copy(scan, way).start)

    def join_offsets(scan, own, lead, first_of_pair, way):
        off_copy(scan, own).wait_recv()
        for j in range(half):
            _, after = in_order(scan["map"][base + j], scan["mate_map"][j], lead)
            one, two = in_order(own[base + j], scan["mate_off"][j], lead)
            scan["chip_off"][j] = two + apply_map(one, *halves(after))
            scan["one_off"][j] = one
            pl.when(first_of_pair)(pair_off_copy(scan, j, way).start)

    def hop_copy(scan, j, to, far):
        at = 3 + 3 * half + j if far else 2 + j
        return remote(
            scan["out"].at[j], scan["arrived"].at[j],
            scan["sem"].at[0, at], scan["sem"].at[1, 2 + j], {"tm": to},
        )

    def hand_copy(scan, j, at):
        return remote(
            scan["hand"].at[j], scan["into"].at[at + j],
            scan["sem"].at[0, 2 + half + j], scan["sem"].at[1, 2 + half + j], {"tm": mate},
        )

    def chain(scan, first, last, lead, first_of_pair, way):
        second = jnp.logical_not(first_of_pair)
        later = jnp.logical_not(first)

        @pl.when(jnp.logical_and(second, later))
        def _():
            pair_map_copy(scan, way).wait_recv()

        for j in range(half):

            @pl.when(second)
            def _():
                pair_off_copy(scan, j, way).wait_recv()
                scan["chip_in"][j] = scan["ahead_off"][j]

            @pl.when(jnp.logical_and(first_of_pair, first))
            def _():
                scan["chip_in"][j] = jnp.zeros((rows, sub), F32)

            pl.when(later)(hop_copy(scan, j, mate, False).wait_recv)

            @pl.when(jnp.logical_and(first_of_pair, later))
            def _():
                scan["chip_in"][j] = scan["arrived"][j]

            @pl.when(jnp.logical_and(second, later))
            def _():
                scan["chip_in"][j] += apply_map(scan["arrived"][j], *halves(scan["ahead_map"][j]))

            @pl.when(jnp.logical_and(second, jnp.logical_not(last)))
            def _():
                after = apply_map(scan["chip_in"][j], scan["chip_h"][j], scan["chip_l"][j])
                scan["out"][j] = scan["chip_off"][j] + after
                hop_copy(scan, j, away(way, 4), True).start()
                hop_copy(scan, j, away(way, 2), False).start()

        for j in range(half):
            chip_in = scan["chip_in"][j]
            after = apply_map(chip_in, scan["one_h"][j], scan["one_l"][j])
            mine, theirs = in_order(chip_in, scan["one_off"][j] + after, lead)
            if split:
                scan["hand"][j] = theirs
                hand_copy(scan, j, base).start()
            scan["into"][base + j] = mine

        @pl.when(jnp.logical_and(second, first))
        def _():
            pair_map_copy(scan, way).wait_recv()

    def scan_end(scan, own, last, first_of_pair, way):
        map_copy(scan).wait_send()
        off_copy(scan, own).wait_send()

        @pl.when(first_of_pair)
        def _():
            pair_map_copy(scan, way).wait_send()
            for j in range(half):
                pair_off_copy(scan, j, way).wait_send()

        @pl.when(jnp.logical_not(jnp.logical_or(first_of_pair, last)))
        def _():
            for j in range(half):
                hop_copy(scan, j, away(way, 4), True).wait_send()
                hop_copy(scan, j, away(way, 2), False).wait_send()

        if split:
            for j in range(half):
                hand_copy(scan, j, base).wait_send()

    f_first, f_last = chip // 2 == 0, chip // 2 == chips // 2 - 1
    b_first, b_last = f_last, f_first
    f_lead, b_lead = lax.rem(chip, 2) == 0, lax.rem(chip, 2) == 1

    up, down = list(range(T)), list(range(T - 1, -1, -1))
    section_maps(((fc, up, fmap_h, fmap_l, f_scan["map"]), (bc, down, bmap_h, bmap_l, b_scan["map"])))
    carry = [None] * nsub
    for t in range(T):
        loads[t].wait()
        full = dot(rs[t], diag[t], ((1,), (1,)))
        for n in range(nsub):
            new = full[:, cols(n)]
            if t > 0:
                new = select(t, new - couple(carry[n], fc[t, cols(n), :]), carry[n])
            carry[n] = new
            driven[t, n] = new
    pl.semaphore_wait(barrier, n_tm - 1 + n_sp - 1)
    map_copy(f_scan).start()
    off_copy(f_scan, driven.at[T - 1]).start()
    map_copy(b_scan).start()
    map_copy(f_scan).wait_recv()
    join_offsets(f_scan, driven.at[T - 1], 0, f_lead, 1)
    join_maps(f_scan, 0, f_lead, 1)

    def early():
        for q in range(n_sp - 1):

            @pl.when(p > q)
            def _():
                for t in range(T):
                    full = dot(arrow[t], diag[t, :, q * width : (q + 1) * width], ((1,), (0,)))
                    for n in range(nsub):
                        v_send[q, t, n] = full[:, cols(n)]
                remote(v_send.at[q], v_recv.at[p - 1], vs_sem.at[q], vr_sem.at[p - 1], {"space": q}).start()

    pl.when(chip >= chips // 2)(early)

    chain(f_scan, f_first, f_last, 0, f_lead, 1)

    if split:
        for j in range(half):
            hand_copy(f_scan, j, other_base).wait_recv()

    merging = n_sp == 4 and nsub % 2 == 0
    mid = nsub // 2

    def product(q, t):
        full = folded(dot(f_split[t], diag[t, :, q * width : (q + 1) * width], ((1,), (0,))))
        for n in range(nsub):
            w_send[q, t, n] = full[:, cols(n)]

    def piece(h):
        return pl.ds(0, nsub) if h is None else pl.ds(h * mid, mid)

    def final(q, t, slot, h):
        sem = h or 0
        return remote(
            w_send.at[q, t, piece(h)], w_recv.at[slot, t, piece(h)],
            ws_sem.at[q, t, sem], wr_sem.at[slot, t, sem], {"space": q},
        )

    def passing(q, t, to, h):
        return remote(
            w_send.at[q, t, piece(h)], w_pass.at[t, piece(h)],
            ps_sem.at[t, h or 0], pr_sem.at[t], {"space": to},
        )

    def merge(q, t, h):
        passing(q, t, 0, h).wait_recv()
        for n in range(nsub) if h is None else range(h * mid, h * mid + mid):
            w_send[q, t, n] += w_pass[t, n]

    for t in down:
        for n in range(nsub):
            state = driven[t, n] + apply_map(f_scan["into"][n], fmap_h[n, :, cols(t)], fmap_l[n, :, cols(t)])
            state = select(t, state, jnp.zeros_like(state))
            f_split[t, :, cols(n)] = stacked(state)

        if merging:

            @pl.when(p == 3)
            def _():
                product(0, t)
                passing(0, t, 2, 0).start()
                passing(0, t, 1, 1).start()

            @pl.when(p == 2)
            def _():
                product(1, t)
                passing(1, t, 3, None).start()
                product(0, t)
                final(0, t, 1, 1).start()

            @pl.when(p == 1)
            def _():
                product(0, t)
                final(0, t, 0, 0).start()

        else:
            for q in range(n_sp - 1):

                @pl.when(p > q)
                def _():
                    product(q, t)
                    final(q, t, p - 1, None).start()

    if merging:

        @pl.when(p == 3)
        def _():
            for t in down:
                product(2, t)
                final(2, t, 0, None).start()
                product(1, t)
                merge(1, t, None)
                final(1, t, 0, None).start()

        @pl.when(p == 2)
        def _():
            for t in down:
                merge(0, t, 0)
                final(0, t, 1, 0).start()

        @pl.when(p == 1)
        def _():
            for t in down:
                merge(0, t, 1)
                final(0, t, 0, 1).start()

    total = jnp.zeros((F, 2 * rows), F32)
    for t in range(T):
        total = total + dot(arrow[t], f_split[t], ((1,), (1,)))
    part[...] = total
    gath_sp[p] = total
    for d in range(1, n_sp):
        remote(part, gath_sp.at[p], as_sem.at[d - 1], ar_sem.at[p], {"space": lax.rem(p + d, n_sp)}).start()

    pl.when(chip < chips // 2)(early)
    map_copy(b_scan).wait_recv()
    join_maps(b_scan, 1, b_lead, -1)

    own_cols = pl.ds(pl.multiple_of(p * width, width), width)
    for t in range(T):
        block = diag[t, :, own_cols]
        full = folded(dot(f_split[t], block, ((1,), (0,))))
        arrow_full = dot(arrow[t], block, ((1,), (0,)))
        for n in range(nsub):
            g_loc[t, n] = full[:, cols(n)]
            v_own[t, n] = arrow_full[:, cols(n)]

    for d in range(1, n_sp):
        come = lax.rem(p + d, n_sp)
        remote(part, gath_sp.at[come], as_sem.at[d - 1], ar_sem.at[come], {"space": come}).wait_recv()
    total = gath_sp[0]
    for i in range(1, n_sp):
        total = total + gath_sp[i]
    mine_tm[...] = total
    gath_tm[s] = total
    for d in range(1, n_tm):
        remote(mine_tm, gath_tm.at[s], ts_sem.at[d - 1], tr_sem.at[s], {"tm": lax.rem(s + d, n_tm)}).start()

    for q in range(1, n_sp):

        @pl.when(p < q)
        def _():
            remote(v_send.at[0], v_recv.at[q - 1], vs_sem.at[0], vr_sem.at[q - 1], {"space": q}).wait_recv()
            for t in range(T):
                for n in range(nsub):
                    v_own[t, n] += v_recv[q - 1, t, n]

    for d in range(1, n_tm):
        come = lax.rem(s + d, n_tm)
        remote(mine_tm, gath_tm.at[come], ts_sem.at[d - 1], tr_sem.at[come], {"tm": come}).wait_recv()
    total = gath_tm[0]
    for i in range(1, n_tm):
        total = total + gath_tm[i]
    exact = functools.partial(
        lax.dot_general, preferred_element_type=F32, precision=lax.Precision.HIGHEST
    )
    side = tip_side[...] - total[:, :rows]
    tip_state = exact(tip_inv[...], side, (((1,), (0,)), ((), ())))
    turned = exact(tip_inv[...].T, tip_state, (((1,), (0,)), ((), ())))
    tip_out[...] = turned
    tip = turned.T

    for t in range(T):
        for n in range(nsub):
            g_loc[t, n] -= exact(tip, v_own[t, n], (((1,), (0,)), ((), ())))

    def take(t, slot, parts):
        for h in parts:
            final(0, t, slot, h).wait_recv()
        for n in range(nsub):
            g_loc[t, n] += w_recv[slot, t, n]

    for t in down:
        if merging:

            @pl.when(p == 0)
            def _():
                take(t, 0, (0, 1))
                take(t, 1, (0, 1))

            @pl.when(jnp.logical_or(p == 1, p == 2))
            def _():
                take(t, 0, (None,))

        else:
            for q in range(1, n_sp):
                pl.when(p < q)(functools.partial(take, t, q - 1, (None,)))

        for n in range(nsub):
            new = g_loc[t, n]
            if t < T - 1:
                old = g_loc[t + 1, n]
                new = select(t, new - couple(old, bc[t, cols(n), :]), old)
            else:
                new = select(t, new, jnp.zeros_like(new))
            g_loc[t, n] = new

    off_copy(b_scan, g_loc.at[0]).start()
    join_offsets(b_scan, g_loc.at[0], 1, b_lead, -1)
    chain(b_scan, b_first, b_last, 1, b_lead, -1)

    if split:
        for j in range(half):
            hand_copy(b_scan, j, other_base).wait_recv()
    for n in range(nsub):
        states = apply_map(b_scan["into"][n], bmap_h[n], bmap_l[n])
        for t in range(T):
            sol[t, :, cols(n)] = g_loc[t, n] + states[:, cols(t)]

    scan_end(f_scan, driven.at[T - 1], f_last, f_lead, 1)
    scan_end(b_scan, g_loc.at[0], b_last, b_lead, -1)
    for q in range(n_sp - 1):

        @pl.when(p > q)
        def _():
            remote(v_send.at[q], v_recv.at[p - 1], vs_sem.at[q], vr_sem.at[p - 1], {"space": q}).wait_send()
            if not merging:
                for t in down:
                    final(q, t, p - 1, None).wait_send()

    if merging:

        @pl.when(p == 3)
        def _():
            for t in down:
                passing(0, t, 2, 0).wait_send()
                passing(0, t, 1, 1).wait_send()
                final(2, t, 0, None).wait_send()
                final(1, t, 0, None).wait_send()

        @pl.when(p == 2)
        def _():
            for t in down:
                passing(1, t, 3, None).wait_send()
                final(0, t, 1, 0).wait_send()
                final(0, t, 1, 1).wait_send()

        @pl.when(p == 1)
        def _():
            for t in down:
                final(0, t, 0, 0).wait_send()
                final(0, t, 0, 1).wait_send()

    for d in range(1, n_sp):
        remote(part, gath_sp.at[p], as_sem.at[d - 1], ar_sem.at[p], {"space": lax.rem(p + d, n_sp)}).wait_send()
    for d in range(1, n_tm):
        remote(mine_tm, gath_tm.at[s], ts_sem.at[d - 1], tr_sem.at[s], {"tm": lax.rem(s + d, n_tm)}).wait_send()


def finish(sec, states, turned, sol, tip):
    length = sec[lax.axis_index("tm")]
    for t in range(states.shape[0]):
        live = jnp.full(states.shape[1:], length, jnp.int32) > t
        sol[t] = jnp.where(live, states[t], jnp.zeros_like(states[t]))
    tip[...] = turned[...]


def scan_scratch(nsub, rows, sub):
    half = nsub // 2 if nsub % 2 == 0 else nsub
    return {
        "map": pltpu.VMEM((nsub, sub, sub), F32),
        "mate_map": pltpu.VMEM((half, sub, sub), F32),
        "chip_map": pltpu.VMEM((half, sub, sub), F32),
        "chip_h": pltpu.VMEM((half, sub, sub), BF16),
        "chip_l": pltpu.VMEM((half, sub, sub), BF16),
        "one_h": pltpu.VMEM((half, sub, sub), BF16),
        "one_l": pltpu.VMEM((half, sub, sub), BF16),
        "ahead_map": pltpu.VMEM((half, sub, sub), F32),
        "mate_off": pltpu.VMEM((half, rows, sub), F32),
        "chip_off": pltpu.VMEM((half, rows, sub), F32),
        "one_off": pltpu.VMEM((half, rows, sub), F32),
        "ahead_off": pltpu.VMEM((half, rows, sub), F32),
        "chip_in": pltpu.VMEM((half, rows, sub), F32),
        "arrived": pltpu.VMEM((half, rows, sub), F32),
        "out": pltpu.VMEM((half, rows, sub), F32),
        "hand": pltpu.VMEM((half, rows, sub), F32),
        "into": pltpu.VMEM((nsub, rows, sub), F32),
        "sem": pltpu.SemaphoreType.DMA((2, 3 + 4 * half)),
    }


def on_device(n_tm, n_sp, sections, right_side, tip_side, diag_inverse, fwd, bwd, arrow_rows, tip_inverse):
    T, rows, total_width = right_side.shape
    width, sub = fwd.shape[1], fwd.shape[2]
    nsub = width // sub
    F = arrow_rows.shape[1]
    vmem, hbm = pl.BlockSpec(memory_space=pltpu.VMEM), pl.BlockSpec(memory_space=pl.ANY)
    maps = pltpu.VMEM((nsub, sub, T * sub), BF16)
    dma = pltpu.SemaphoreType.DMA
    others = n_sp - 1
    states, turned = pl.pallas_call(
        functools.partial(kernel, n_tm, n_sp),
        out_shape=(
            jax.ShapeDtypeStruct((T, rows, width), F32),
            jax.ShapeDtypeStruct(tip_side.shape[::-1], F32),
        ),
        in_specs=[
            pl.BlockSpec(memory_space=pltpu.SMEM),
            vmem,
            vmem,
            hbm,
            vmem,
            vmem,
            vmem,
            vmem,
        ],
        out_specs=(vmem, vmem),
        scratch_shapes=[
            pltpu.VMEM(diag_inverse.shape, BF16),
            maps,
            maps,
            maps,
            maps,
            pltpu.VMEM((T, nsub, rows, sub), F32),
            pltpu.VMEM((T, 2 * rows, width), BF16),
            pltpu.VMEM((T, nsub, rows, sub), F32),
            pltpu.VMEM((others, T, nsub, rows, sub), F32),
            pltpu.VMEM((others, T, nsub, rows, sub), F32),
            pltpu.VMEM((T, nsub, rows, sub), F32),
            pltpu.VMEM((others, T, nsub, F, sub), F32),
            pltpu.VMEM((others, T, nsub, F, sub), F32),
            pltpu.VMEM((T, nsub, F, sub), F32),
            pltpu.VMEM((F, 2 * rows), F32),
            pltpu.VMEM((n_sp, F, 2 * rows), F32),
            pltpu.VMEM((n_tm, F, 2 * rows), F32),
            pltpu.VMEM((F, 2 * rows), F32),
            scan_scratch(nsub, rows, sub),
            scan_scratch(nsub, rows, sub),
            dma((T,)),
            dma((others, T, 2)),
            dma((others, T, 2)),
            dma((T, 2)),
            dma((T,)),
            dma((others,)),
            dma((others,)),
            dma((others,)),
            dma((n_sp,)),
            dma((n_tm - 1,)),
            dma((n_tm,)),
        ],
        compiler_params=pltpu.CompilerParams(
            collective_id=0, has_side_effects=True, vmem_limit_bytes=56 * 1024 * 1024
        ),
        cost_estimate=pl.CostEstimate(
            flops=8 * T * rows * width * total_width, bytes_accessed=2 * diag_inverse.size, transcendentals=0
        ),
    )(sections, right_side, tip_side.T, diag_inverse, fwd, bwd, arrow_rows, tip_inverse)
    states, turned = pl.pallas_call(
        finish,
        out_shape=(
            jax.ShapeDtypeStruct(states.shape, F32),
            jax.ShapeDtypeStruct(turned.shape, F32),
        ),
        in_specs=[pl.BlockSpec(memory_space=pltpu.SMEM), vmem, vmem],
        out_specs=(vmem, vmem),
    )(sections, states, turned)
    return states, turned.T


def solution(mesh):
    placed = (
        P(),
        P("tm", None, None),
        P(),
        P("tm", "space", None),
        P("tm", "space", None),
        P("tm", "space", None),
        P("tm", None, "space"),
        P(),
    )
    return jax.shard_map(
        functools.partial(on_device, mesh.shape["tm"], mesh.shape["space"]),
        mesh=mesh,
        in_specs=placed,
        out_specs=(P("tm", None, "space"), P()),
        check_vma=False,
    )
```

```python
import functools

import jax
import jax.numpy as jnp
from jax import lax
from jax.experimental import pallas as pl
from jax.experimental.pallas import tpu as pltpu
from jax.sharding import PartitionSpec as P

F32 = jnp.float32
BF16 = jnp.bfloat16
MESH = pl.DeviceIdType.MESH


def dot(a, b, contract):
    return lax.dot_general(a, b, (contract, ((), ())), preferred_element_type=F32)


def stacked(x):
    high = x.astype(BF16).astype(F32)
    return jnp.concatenate([high, x - high], 0).astype(BF16)


def folded(y):
    rows = y.shape[0] // 2
    return y[:rows] + y[rows:]


def couple(x, block):
    return folded(dot(stacked(x), block, ((1,), (1,))))


def halves(x):
    high = x.astype(BF16)
    return high, (x - high.astype(F32)).astype(BF16)


def apply_map(x, high, low):
    rows = x.shape[0]
    pieces = stacked(x)
    return folded(dot(pieces, high, ((1,), (0,)))) + dot(pieces[:rows], low, ((1,), (0,)))


def kernel(
    n_tm, n_sp, sec, rs, tip_side, diag_hbm, fc, bc, arrow, tip_inv,
    sol, tip_out,
    diag, fmap_h, fmap_l, bmap_h, bmap_l, driven, f_split, g_loc,
    w_send, w_recv, w_pass, v_send, v_recv, v_own, part, gath_sp, gath_tm, mine_tm,
    f_scan, b_scan,
    diag_sem, ws_sem, wr_sem, ps_sem, pr_sem, vs_sem, vr_sem, as_sem, ar_sem, ts_sem, tr_sem,
):
    T, rows = rs.shape[0], rs.shape[1]
    width, sub = fc.shape[1], fc.shape[2]
    nsub = width // sub
    F = arrow.shape[1]
    s, p = lax.axis_index("tm"), lax.axis_index("space")
    core, chip, chips = lax.rem(s, 2), s // 2, n_tm // 2
    length = sec[s]
    half, split = (nsub // 2, True) if nsub % 2 == 0 else (nsub, False)
    base = core * half if split else 0
    other_base = half - core * half if split else 0
    mate = s + 1 - 2 * core

    loads = [
        pltpu.make_async_copy(diag_hbm.at[t], diag.at[t], diag_sem.at[t]) for t in range(T)
    ]
    for load in loads:
        load.start()

    barrier = pltpu.get_barrier_semaphore()
    for d in range(1, n_tm):
        pl.semaphore_signal(barrier, inc=1, device_id={"tm": lax.rem(s + d, n_tm)}, device_id_type=MESH)
    for d in range(1, n_sp):
        pl.semaphore_signal(barrier, inc=1, device_id={"space": lax.rem(p + d, n_sp)}, device_id_type=MESH)

    def cols(n):
        return slice(n * sub, (n + 1) * sub)

    def select(t, new, old):
        if t == 0:
            return new
        return jnp.where(jnp.full(new.shape, length, jnp.int32) > t, new, old)

    def remote(src, dst, send, recv, to):
        return pltpu.make_async_remote_copy(
            src_ref=src, dst_ref=dst, send_sem=send, recv_sem=recv, device_id=to, device_id_type=MESH
        )

    def section_maps(jobs):
        row = lax.broadcasted_iota(jnp.int32, (sub, sub), 0)
        col = lax.broadcasted_iota(jnp.int32, (sub, sub), 1)
        eye = jnp.where(row == col, 1.0, 0.0)
        maps = [[eye.astype(F32)] * nsub for _ in jobs]
        for i in range(T):
            for own, (coupling, order, high_ref, low_ref, _) in zip(maps, jobs):
                t = order[i]
                for n in range(nsub):
                    block = coupling[t, cols(n), :]
                    if i == 0:
                        new = -dot(eye.astype(BF16), block, ((1,), (1,)))
                    else:
                        new = -couple(own[n], block)
                    own[n] = select(t, new, own[n])
                    high_ref[n, :, cols(t)], low_ref[n, :, cols(t)] = halves(own[n])
        for own, job in zip(maps, jobs):
            for n in range(nsub):
                job[4][n] = own[n]

    def in_order(mine, theirs, lead):
        ahead = jnp.full(mine.shape, core, jnp.int32) == lead
        return jnp.where(ahead, mine, theirs), jnp.where(ahead, theirs, mine)

    def map_copy(scan):
        return remote(
            scan["map"].at[pl.ds(other_base, half)], scan["mate_map"],
            scan["sem"].at[0, 0], scan["sem"].at[1, 0], {"tm": mate},
        )

    def off_copy(scan, own):
        return remote(
            own.at[pl.ds(other_base, half)], scan["mate_off"],
            scan["sem"].at[0, 1], scan["sem"].at[1, 1], {"tm": mate},
        )

    def pair_map_copy(scan, way):
        return remote(
            scan["chip_map"], scan["ahead_map"],
            scan["sem"].at[0, 2 + 2 * half], scan["sem"].at[1, 2 + 2 * half], {"tm": away(way, 2)},
        )

    def pair_off_copy(scan, j, way):
        at = 3 + 2 * half + j
        return remote(
            scan["chip_off"].at[j], scan["ahead_off"].at[j],
            scan["sem"].at[0, at], scan["sem"].at[1, at], {"tm": away(way, 2)},
        )

    def away(way, steps):
        return lax.rem(s + n_tm + way * steps, n_tm)

    def join_maps(scan, lead, first, first_of_pair, way):
        for j in range(half):
            one, two = in_order(scan["map"][base + j], scan["mate_map"][j], lead)
            scan["one_h"][j], scan["one_l"][j] = halves(one)
            both = apply_map(one, *halves(two))
            scan["chip_map"][j] = both
            scan["chip_h"][j], scan["chip_l"][j] = halves(both)
        pl.when(jnp.logical_and(first_of_pair, jnp.logical_not(first)))(pair_map_copy(scan, way).start)

    def join_offsets(scan, own, lead, first_of_pair, way):
        off_copy(scan, own).wait_recv()
        for j in range(half):
            _, after = in_order(scan["map"][base + j], scan["mate_map"][j], lead)
            one, two = in_order(own[base + j], scan["mate_off"][j], lead)
            scan["chip_off"][j] = two + apply_map(one, *halves(after))
            scan["one_off"][j] = one
            pl.when(first_of_pair)(pair_off_copy(scan, j, way).start)

    def hop_copy(scan, j, to, far):
        at = 3 + 3 * half + j if far else 2 + j
        return remote(
            scan["out"].at[j], scan["arrived"].at[j],
            scan["sem"].at[0, at], scan["sem"].at[1, 2 + j], {"tm": to},
        )

    def hand_copy(scan, j, at):
        return remote(
            scan["hand"].at[j], scan["into"].at[at + j],
            scan["sem"].at[0, 2 + half + j], scan["sem"].at[1, 2 + half + j], {"tm": mate},
        )

    def chain(scan, first, last, lead, first_of_pair, way):
        second = jnp.logical_not(first_of_pair)
        later = jnp.logical_not(first)

        @pl.when(jnp.logical_and(second, later))
        def _():
            pair_map_copy(scan, way).wait_recv()

        for j in range(half):

            @pl.when(second)
            def _():
                pair_off_copy(scan, j, way).wait_recv()
                scan["chip_in"][j] = scan["ahead_off"][j]

            @pl.when(jnp.logical_and(first_of_pair, first))
            def _():
                scan["chip_in"][j] = jnp.zeros((rows, sub), F32)

            pl.when(later)(hop_copy(scan, j, mate, False).wait_recv)

            @pl.when(jnp.logical_and(first_of_pair, later))
            def _():
                scan["chip_in"][j] = scan["arrived"][j]

            @pl.when(jnp.logical_and(second, later))
            def _():
                scan["chip_in"][j] += apply_map(scan["arrived"][j], *halves(scan["ahead_map"][j]))

            @pl.when(jnp.logical_and(second, jnp.logical_not(last)))
            def _():
                after = apply_map(scan["chip_in"][j], scan["chip_h"][j], scan["chip_l"][j])
                scan["out"][j] = scan["chip_off"][j] + after
                hop_copy(scan, j, away(way, 4), True).start()
                hop_copy(scan, j, away(way, 2), False).start()

        for j in range(half):
            chip_in = scan["chip_in"][j]
            after = apply_map(chip_in, scan["one_h"][j], scan["one_l"][j])
            mine, theirs = in_order(chip_in, scan["one_off"][j] + after, lead)
            if split:
                scan["hand"][j] = theirs
                hand_copy(scan, j, base).start()
            scan["into"][base + j] = mine

    def scan_end(scan, own, first, last, first_of_pair, way):
        map_copy(scan).wait_send()
        off_copy(scan, own).wait_send()

        pl.when(jnp.logical_and(first_of_pair, jnp.logical_not(first)))(pair_map_copy(scan, way).wait_send)

        @pl.when(first_of_pair)
        def _():
            for j in range(half):
                pair_off_copy(scan, j, way).wait_send()

        @pl.when(jnp.logical_not(jnp.logical_or(first_of_pair, last)))
        def _():
            for j in range(half):
                hop_copy(scan, j, away(way, 4), True).wait_send()
                hop_copy(scan, j, away(way, 2), False).wait_send()

        if split:
            for j in range(half):
                hand_copy(scan, j, base).wait_send()

    f_first, f_last = chip // 2 == 0, chip // 2 == chips // 2 - 1
    b_first, b_last = f_last, f_first
    f_lead, b_lead = lax.rem(chip, 2) == 0, lax.rem(chip, 2) == 1

    up, down = list(range(T)), list(range(T - 1, -1, -1))
    section_maps(((fc, up, fmap_h, fmap_l, f_scan["map"]), (bc, down, bmap_h, bmap_l, b_scan["map"])))
    carry = [None] * nsub
    for t in range(T):
        loads[t].wait()
        full = dot(rs[t], diag[t], ((1,), (1,)))
        for n in range(nsub):
            new = full[:, cols(n)]
            if t > 0:
                new = select(t, new - couple(carry[n], fc[t, cols(n), :]), carry[n])
            carry[n] = new
            driven[t, n] = new
    pl.semaphore_wait(barrier, n_tm - 1 + n_sp - 1)
    map_copy(f_scan).start()
    off_copy(f_scan, driven.at[T - 1]).start()
    map_copy(b_scan).start()

    def early():
        for q in range(n_sp - 1):

            @pl.when(p > q)
            def _():
                for t in range(T):
                    full = dot(arrow[t], diag[t, :, q * width : (q + 1) * width], ((1,), (0,)))
                    for n in range(nsub):
                        v_send[q, t, n] = full[:, cols(n)]
                remote(v_send.at[q], v_recv.at[p - 1], vs_sem.at[q], vr_sem.at[p - 1], {"space": q}).start()

    pl.when(chip >= chips // 2)(early)

    map_copy(f_scan).wait_recv()
    join_offsets(f_scan, driven.at[T - 1], 0, f_lead, 1)
    join_maps(f_scan, 0, f_first, f_lead, 1)

    chain(f_scan, f_first, f_last, 0, f_lead, 1)

    if split:
        for j in range(half):
            hand_copy(f_scan, j, other_base).wait_recv()

    merging = n_sp == 4 and nsub % 2 == 0
    mid = nsub // 2

    def product(q, t):
        full = folded(dot(f_split[t], diag[t, :, q * width : (q + 1) * width], ((1,), (0,))))
        for n in range(nsub):
            w_send[q, t, n] = full[:, cols(n)]

    def piece(h):
        return pl.ds(0, nsub) if h is None else pl.ds(h * mid, mid)

    def final(q, t, slot, h):
        sem = h or 0
        return remote(
            w_send.at[q, t, piece(h)], w_recv.at[slot, t, piece(h)],
            ws_sem.at[q, t, sem], wr_sem.at[slot, t, sem], {"space": q},
        )

    def passing(q, t, to, h):
        return remote(
            w_send.at[q, t, piece(h)], w_pass.at[t, piece(h)],
            ps_sem.at[t, h or 0], pr_sem.at[t], {"space": to},
        )

    def merge(q, t, h):
        passing(q, t, 0, h).wait_recv()
        for n in range(nsub) if h is None else range(h * mid, h * mid + mid):
            w_send[q, t, n] += w_pass[t, n]

    for t in down:
        for n in range(nsub):
            state = driven[t, n] + apply_map(f_scan["into"][n], fmap_h[n, :, cols(t)], fmap_l[n, :, cols(t)])
            state = select(t, state, jnp.zeros_like(state))
            f_split[t, :, cols(n)] = stacked(state)

        if merging:

            @pl.when(p == 3)
            def _():
                product(0, t)
                passing(0, t, 2, 0).start()
                passing(0, t, 1, 1).start()

            @pl.when(p == 2)
            def _():
                product(1, t)
                passing(1, t, 3, None).start()
                product(0, t)
                final(0, t, 1, 1).start()

            @pl.when(p == 1)
            def _():
                product(0, t)
                final(0, t, 0, 0).start()

        else:
            for q in range(n_sp - 1):

                @pl.when(p > q)
                def _():
                    product(q, t)
                    final(q, t, p - 1, None).start()

    if merging:

        @pl.when(p == 3)
        def _():
            for t in down:
                product(2, t)
                final(2, t, 0, None).start()
                product(1, t)
                merge(1, t, None)
                final(1, t, 0, None).start()

        @pl.when(p == 2)
        def _():
            for t in down:
                merge(0, t, 0)
                final(0, t, 1, 0).start()

        @pl.when(p == 1)
        def _():
            for t in down:
                merge(0, t, 1)
                final(0, t, 0, 1).start()

    total = jnp.zeros((F, 2 * rows), F32)
    for t in range(T):
        total = total + dot(arrow[t], f_split[t], ((1,), (1,)))
    part[...] = total
    gath_sp[p] = total
    for d in range(1, n_sp):
        remote(part, gath_sp.at[p], as_sem.at[d - 1], ar_sem.at[p], {"space": lax.rem(p + d, n_sp)}).start()

    pl.when(chip < chips // 2)(early)
    map_copy(b_scan).wait_recv()
    join_maps(b_scan, 1, b_first, b_lead, -1)

    own_cols = pl.ds(pl.multiple_of(p * width, width), width)
    for t in range(T):
        block = diag[t, :, own_cols]
        full = folded(dot(f_split[t], block, ((1,), (0,))))
        arrow_full = dot(arrow[t], block, ((1,), (0,)))
        for n in range(nsub):
            g_loc[t, n] = full[:, cols(n)]
            v_own[t, n] = arrow_full[:, cols(n)]

    for d in range(1, n_sp):
        come = lax.rem(p + d, n_sp)
        remote(part, gath_sp.at[come], as_sem.at[d - 1], ar_sem.at[come], {"space": come}).wait_recv()
    total = gath_sp[0]
    for i in range(1, n_sp):
        total = total + gath_sp[i]
    mine_tm[...] = total
    gath_tm[s] = total
    for d in range(1, n_tm):
        remote(mine_tm, gath_tm.at[s], ts_sem.at[d - 1], tr_sem.at[s], {"tm": lax.rem(s + d, n_tm)}).start()

    for q in range(1, n_sp):

        @pl.when(p < q)
        def _():
            remote(v_send.at[0], v_recv.at[q - 1], vs_sem.at[0], vr_sem.at[q - 1], {"space": q}).wait_recv()
            for t in range(T):
                for n in range(nsub):
                    v_own[t, n] += v_recv[q - 1, t, n]

    for d in range(1, n_tm):
        come = lax.rem(s + d, n_tm)
        remote(mine_tm, gath_tm.at[come], ts_sem.at[d - 1], tr_sem.at[come], {"tm": come}).wait_recv()
    total = gath_tm[0]
    for i in range(1, n_tm):
        total = total + gath_tm[i]
    exact = functools.partial(
        lax.dot_general, preferred_element_type=F32, precision=lax.Precision.HIGHEST
    )
    side = tip_side[...] - total[:, :rows]
    tip_state = exact(tip_inv[...], side, (((1,), (0,)), ((), ())))
    turned = exact(tip_inv[...].T, tip_state, (((1,), (0,)), ((), ())))
    tip_out[...] = turned
    tip = turned.T

    for t in range(T):
        for n in range(nsub):
            g_loc[t, n] -= exact(tip, v_own[t, n], (((1,), (0,)), ((), ())))

    def take(t, slot, parts):
        for h in parts:
            final(0, t, slot, h).wait_recv()
        for n in range(nsub):
            g_loc[t, n] += w_recv[slot, t, n]

    for t in down:
        if merging:

            @pl.when(p == 0)
            def _():
                take(t, 0, (0, 1))
                take(t, 1, (0, 1))

            @pl.when(jnp.logical_or(p == 1, p == 2))
            def _():
                take(t, 0, (None,))

        else:
            for q in range(1, n_sp):
                pl.when(p < q)(functools.partial(take, t, q - 1, (None,)))

        for n in range(nsub):
            new = g_loc[t, n]
            if t < T - 1:
                old = g_loc[t + 1, n]
                new = select(t, new - couple(old, bc[t, cols(n), :]), old)
            else:
                new = select(t, new, jnp.zeros_like(new))
            g_loc[t, n] = new

    off_copy(b_scan, g_loc.at[0]).start()
    join_offsets(b_scan, g_loc.at[0], 1, b_lead, -1)
    chain(b_scan, b_first, b_last, 1, b_lead, -1)

    if split:
        for j in range(half):
            hand_copy(b_scan, j, other_base).wait_recv()
    for n in range(nsub):
        states = apply_map(b_scan["into"][n], bmap_h[n], bmap_l[n])
        for t in range(T):
            sol[t, :, cols(n)] = g_loc[t, n] + states[:, cols(t)]

    scan_end(f_scan, driven.at[T - 1], f_first, f_last, f_lead, 1)
    scan_end(b_scan, g_loc.at[0], b_first, b_last, b_lead, -1)
    for q in range(n_sp - 1):

        @pl.when(p > q)
        def _():
            remote(v_send.at[q], v_recv.at[p - 1], vs_sem.at[q], vr_sem.at[p - 1], {"space": q}).wait_send()
            if not merging:
                for t in down:
                    final(q, t, p - 1, None).wait_send()

    if merging:

        @pl.when(p == 3)
        def _():
            for t in down:
                passing(0, t, 2, 0).wait_send()
                passing(0, t, 1, 1).wait_send()
                final(2, t, 0, None).wait_send()
                final(1, t, 0, None).wait_send()

        @pl.when(p == 2)
        def _():
            for t in down:
                passing(1, t, 3, None).wait_send()
                final(0, t, 1, 0).wait_send()
                final(0, t, 1, 1).wait_send()

        @pl.when(p == 1)
        def _():
            for t in down:
                final(0, t, 0, 0).wait_send()
                final(0, t, 0, 1).wait_send()

    for d in range(1, n_sp):
        remote(part, gath_sp.at[p], as_sem.at[d - 1], ar_sem.at[p], {"space": lax.rem(p + d, n_sp)}).wait_send()
    for d in range(1, n_tm):
        remote(mine_tm, gath_tm.at[s], ts_sem.at[d - 1], tr_sem.at[s], {"tm": lax.rem(s + d, n_tm)}).wait_send()


def finish(sec, states, turned, sol, tip):
    length = sec[lax.axis_index("tm")]
    for t in range(states.shape[0]):
        live = jnp.full(states.shape[1:], length, jnp.int32) > t
        sol[t] = jnp.where(live, states[t], jnp.zeros_like(states[t]))
    tip[...] = turned[...]


def scan_scratch(nsub, rows, sub):
    half = nsub // 2 if nsub % 2 == 0 else nsub
    return {
        "map": pltpu.VMEM((nsub, sub, sub), F32),
        "mate_map": pltpu.VMEM((half, sub, sub), F32),
        "chip_map": pltpu.VMEM((half, sub, sub), F32),
        "chip_h": pltpu.VMEM((half, sub, sub), BF16),
        "chip_l": pltpu.VMEM((half, sub, sub), BF16),
        "one_h": pltpu.VMEM((half, sub, sub), BF16),
        "one_l": pltpu.VMEM((half, sub, sub), BF16),
        "ahead_map": pltpu.VMEM((half, sub, sub), F32),
        "mate_off": pltpu.VMEM((half, rows, sub), F32),
        "chip_off": pltpu.VMEM((half, rows, sub), F32),
        "one_off": pltpu.VMEM((half, rows, sub), F32),
        "ahead_off": pltpu.VMEM((half, rows, sub), F32),
        "chip_in": pltpu.VMEM((half, rows, sub), F32),
        "arrived": pltpu.VMEM((half, rows, sub), F32),
        "out": pltpu.VMEM((half, rows, sub), F32),
        "hand": pltpu.VMEM((half, rows, sub), F32),
        "into": pltpu.VMEM((nsub, rows, sub), F32),
        "sem": pltpu.SemaphoreType.DMA((2, 3 + 4 * half)),
    }


def on_device(n_tm, n_sp, sections, right_side, tip_side, diag_inverse, fwd, bwd, arrow_rows, tip_inverse):
    T, rows, total_width = right_side.shape
    width, sub = fwd.shape[1], fwd.shape[2]
    nsub = width // sub
    F = arrow_rows.shape[1]
    vmem, hbm = pl.BlockSpec(memory_space=pltpu.VMEM), pl.BlockSpec(memory_space=pl.ANY)
    maps = pltpu.VMEM((nsub, sub, T * sub), BF16)
    dma = pltpu.SemaphoreType.DMA
    others = n_sp - 1
    states, turned = pl.pallas_call(
        functools.partial(kernel, n_tm, n_sp),
        out_shape=(
            jax.ShapeDtypeStruct((T, rows, width), F32),
            jax.ShapeDtypeStruct(tip_side.shape[::-1], F32),
        ),
        in_specs=[
            pl.BlockSpec(memory_space=pltpu.SMEM),
            vmem,
            vmem,
            hbm,
            vmem,
            vmem,
            vmem,
            vmem,
        ],
        out_specs=(vmem, vmem),
        scratch_shapes=[
            pltpu.VMEM(diag_inverse.shape, BF16),
            maps,
            maps,
            maps,
            maps,
            pltpu.VMEM((T, nsub, rows, sub), F32),
            pltpu.VMEM((T, 2 * rows, width), BF16),
            pltpu.VMEM((T, nsub, rows, sub), F32),
            pltpu.VMEM((others, T, nsub, rows, sub), F32),
            pltpu.VMEM((others, T, nsub, rows, sub), F32),
            pltpu.VMEM((T, nsub, rows, sub), F32),
            pltpu.VMEM((others, T, nsub, F, sub), F32),
            pltpu.VMEM((others, T, nsub, F, sub), F32),
            pltpu.VMEM((T, nsub, F, sub), F32),
            pltpu.VMEM((F, 2 * rows), F32),
            pltpu.VMEM((n_sp, F, 2 * rows), F32),
            pltpu.VMEM((n_tm, F, 2 * rows), F32),
            pltpu.VMEM((F, 2 * rows), F32),
            scan_scratch(nsub, rows, sub),
            scan_scratch(nsub, rows, sub),
            dma((T,)),
            dma((others, T, 2)),
            dma((others, T, 2)),
            dma((T, 2)),
            dma((T,)),
            dma((others,)),
            dma((others,)),
            dma((others,)),
            dma((n_sp,)),
            dma((n_tm - 1,)),
            dma((n_tm,)),
        ],
        compiler_params=pltpu.CompilerParams(
            collective_id=0, has_side_effects=True, vmem_limit_bytes=56 * 1024 * 1024
        ),
        cost_estimate=pl.CostEstimate(
            flops=8 * T * rows * width * total_width, bytes_accessed=2 * diag_inverse.size, transcendentals=0
        ),
    )(sections, right_side, tip_side.T, diag_inverse, fwd, bwd, arrow_rows, tip_inverse)
    states, turned = pl.pallas_call(
        finish,
        out_shape=(
            jax.ShapeDtypeStruct(states.shape, F32),
            jax.ShapeDtypeStruct(turned.shape, F32),
        ),
        in_specs=[pl.BlockSpec(memory_space=pltpu.SMEM), vmem, vmem],
        out_specs=(vmem, vmem),
    )(sections, states, turned)
    return states, turned.T


def solution(mesh):
    placed = (
        P(),
        P("tm", None, None),
        P(),
        P("tm", "space", None),
        P("tm", "space", None),
        P("tm", "space", None),
        P("tm", None, "space"),
        P(),
    )
    return jax.shard_map(
        functools.partial(on_device, mesh.shape["tm"], mesh.shape["space"]),
        mesh=mesh,
        in_specs=placed,
        out_specs=(P("tm", None, "space"), P()),
        check_vma=False,
    )
```
